256 devices in a mesh: tm: 64 (over x, y_lo, z), site: 4 (over y_hi, core).
Axes of the slice: x: 4, y: 4 (y_hi: 2, y_lo: 2; y = y_hi * 2 + y_lo), z: 8, core: 2. Of those that a mesh axis runs over, the one named last changes fastest.
Arguments:
- fields: int32 [64, 4096], P('tm', 'site'), may hold values 0 or 1
- bonds: int32 [4, 2048], replicated, may hold values 0 or 1
- source_sites: int32 [128], replicated, may hold values from 0 to 4095
- initial: float32 [64, 4096, 128], P('tm', 'site'), may hold values from -1.2 to 1.2
Outputs:
- solution: float32 [64, 4096, 128], P('tm', 'site')
- gradient: float32 [64, 4096, 128], P('tm', 'site')
The draws below stay inside these ranges and needn't reach their ends.
All inputs are finite; a program needn't handle non-finite values. No bound on the sum of `fields` on one device may be relied on, other than what follows from the above.
Results may differ from the reference program's by a relative error of at most 0.00024.
Values sent between devices are 32-bit elements; how exact they have to be, the bound alone decides.
No kernel may reach another device: no remote copies, remote signals or barrier semaphores. Data moves between devices by JAX's collectives and lax.ppermute only.
A program may use at most 64 MiB of HBM per device.

```python
import jax
import jax.numpy as jnp

LX = 64
LY = 64
N = 4096
PANEL = 128
SLICES = 64
ITERS = 6


def plant(entries, stream_key, least, largest):
    extent = entries.shape
    index_at = [jax.random.randint(jax.random.fold_in(stream_key, axis), (), 0, extent[axis]) for axis in range(len(extent))]
    entries = entries.at[tuple(index_at)].set(least)
    longest = extent.index(max(extent))
    index_at[longest] = (index_at[longest] + 1) % extent[longest]
    return entries.at[tuple(index_at)].set(largest)


def steps_of(key, dims, pieces, smallest, high):
    def one(axis_at, shards_of):
        draws = jax.random.uniform(jax.random.fold_in(jax.random.fold_in(key, 6), axis_at), (shards_of,), jnp.float32, smallest / len(pieces), high / len(pieces))
        return jnp.repeat(jnp.exp(draws), dims[axis_at] // shards_of).reshape((-1,) + (1,) * (len(dims) - axis_at - 1))

    level = one(*pieces[0])
    for cut in pieces[1:]:
        level = level * one(*cut)
    return level


def noise(stream_key, shape, spread, limit, cuts=(), kind=jnp.bfloat16):
    gain = steps_of(stream_key, shape, cuts, -0.22, 0.18) if cuts else 1.0
    values = jax.random.normal(stream_key, shape, jnp.float32) * spread * gain
    return jnp.minimum(jnp.maximum(values, -limit), limit).astype(kind)


def setup_inputs(seed: int = 0) -> dict:
    streams_of = jax.random.split(jax.random.key(seed), 5)
    return {
        "fields": plant((jax.random.randint(streams_of[0], (SLICES, N), 0, 2) < 1).astype(jnp.int32), jax.random.fold_in(streams_of[0], 1), 0, 1),
        "bonds": plant((jax.random.randint(streams_of[1], (4, N // 2), 0, 4) < 3).astype(jnp.int32), jax.random.fold_in(streams_of[1], 1), 0, 1),
        "source_sites": plant(jax.random.randint(streams_of[2], (PANEL,), 0, N), jax.random.fold_in(streams_of[2], 1), 0, N - 1).astype(jnp.int32),
        "initial": noise(streams_of[3], (SLICES, N, PANEL), 0.2, 1.2, ((0, 64), (1, 4)), jnp.float32),
    }


coupling = 0.7368
hop_angle = 0.125


def rotate_pair(former, latter, hyper_cos, hyper_sin):
    return hyper_cos * former + hyper_sin * latter, hyper_sin * former + hyper_cos * latter


def hyper_tables(bonds):
    kept_bonds = bonds.astype(jnp.float32)
    angle_value = jnp.float32(hop_angle)
    return 1.0 + kept_bonds * (jnp.cosh(angle_value) - 1.0), kept_bonds * jnp.sinh(angle_value)


def bond_pairs_x(values, hyper_cos, hyper_sin):
    batch_count, row_count, site_count, column_count = values.shape
    paired = values.reshape(batch_count, row_count, site_count // 2, 2, column_count)
    former, latter = rotate_pair(paired[:, :, :, 0], paired[:, :, :, 1], hyper_cos[None, :, :, None], hyper_sin[None, :, :, None])
    return jnp.stack([former, latter], axis=3).reshape(batch_count, row_count, site_count, column_count)


def shifted_pairs_x(values, hyper_cos, hyper_sin):
    rolled = jnp.roll(values, -1, axis=2)
    return jnp.roll(bond_pairs_x(rolled, hyper_cos, hyper_sin), 1, axis=2)


def bond_pairs_y(values, hyper_cos, hyper_sin):
    batch_count, row_count, site_count, column_count = values.shape
    paired = values.reshape(batch_count, row_count // 2, 2, site_count, column_count)
    former, latter = rotate_pair(paired[:, :, 0], paired[:, :, 1], hyper_cos[None, :, :, None], hyper_sin[None, :, :, None])
    return jnp.stack([former, latter], axis=2).reshape(batch_count, row_count, site_count, column_count)


def shifted_pairs_y(values, hyper_cos, hyper_sin):
    rolled = jnp.roll(values, -1, axis=1)
    return jnp.roll(bond_pairs_y(rolled, hyper_cos, hyper_sin), 1, axis=1)


def apply_slice_matrix(values, growth, tables):
    batch_count, site_total, column_count = values.shape
    lattice = values.reshape(batch_count, LY, LX, column_count) * growth[..., None]
    lattice = bond_pairs_x(lattice, tables[0][0], tables[0][1])
    lattice = shifted_pairs_x(lattice, tables[1][0], tables[1][1])
    lattice = bond_pairs_y(lattice, tables[2][0], tables[2][1])
    lattice = shifted_pairs_y(lattice, tables[3][0], tables[3][1])
    return lattice.reshape(batch_count, site_total, column_count)


def apply_transposed(values, growth, tables):
    batch_count, site_total, column_count = values.shape
    lattice = values.reshape(batch_count, LY, LX, column_count)
    lattice = shifted_pairs_y(lattice, tables[3][0], tables[3][1])
    lattice = bond_pairs_y(lattice, tables[2][0], tables[2][1])
    lattice = shifted_pairs_x(lattice, tables[1][0], tables[1][1])
    lattice = bond_pairs_x(lattice, tables[0][0], tables[0][1])
    lattice = lattice * growth[..., None]
    return lattice.reshape(batch_count, site_total, column_count)


def reference(fields, bonds, source_sites, initial):
    growth = jnp.exp(coupling * (2.0 * fields.astype(jnp.float32) - 1.0)).reshape(SLICES, LY, LX)
    hyper_cos, hyper_sin = hyper_tables(bonds)
    tables = [
        (hyper_cos[0].reshape(LY, LX // 2), hyper_sin[0].reshape(LY, LX // 2)),
        (hyper_cos[1].reshape(LY, LX // 2), hyper_sin[1].reshape(LY, LX // 2)),
        (hyper_cos[2].reshape(LY // 2, LX), hyper_sin[2].reshape(LY // 2, LX)),
        (hyper_cos[3].reshape(LY // 2, LX), hyper_sin[3].reshape(LY // 2, LX)),
    ]
    slice_ids = jnp.arange(SLICES, dtype=jnp.int32)
    column_ids = jnp.arange(PANEL, dtype=jnp.int32)
    site_ids = jnp.arange(N, dtype=jnp.int32)
    source_slice = (column_ids * SLICES) // PANEL
    matches = (slice_ids[:, None, None] == source_slice[None, None, :]) & (site_ids[None, :, None] == source_sites[None, None, :])
    source = matches.astype(jnp.float32)
    own_sign = jnp.where(slice_ids == 0, 1.0, -1.0).astype(jnp.float32)[:, None, None]
    next_sign = jnp.roll(own_sign, -1, axis=0)

    def forward_product(values):
        earlier = jnp.roll(values, 1, axis=0)
        return values + own_sign * apply_slice_matrix(earlier, growth, tables)

    def backward_product(values):
        image_now = apply_transposed(values, growth, tables)
        return values + next_sign * jnp.roll(image_now, -1, axis=0)

    solution = initial
    residual = source - forward_product(initial)
    gradient = backward_product(residual)
    direction = gradient
    gamma_now = jnp.sum(gradient * gradient, axis=(0, 1))
    for iteration in range(ITERS):
        image_now = forward_product(direction)
        step_size = (gamma_now / jnp.sum(image_now * image_now, axis=(0, 1)))[None, None, :]
        solution = solution + step_size * direction
        residual = residual - step_size * image_now
        gradient = backward_product(residual)
        gamma_next = jnp.sum(gradient * gradient, axis=(0, 1))
        direction = gradient + (gamma_next / gamma_now)[None, None, :] * direction
        gamma_now = gamma_next
    return solution, gradient
```

```python
import math

import jax
import jax.numpy as jnp
from jax import lax
from jax.experimental import pallas as pl
from jax.experimental.pallas import tpu as pltpu
from jax.sharding import PartitionSpec as P

LX = 64
LY = 64
PANEL = 128
SLICES = 64
ITERS = 6

coupling = 0.7368
hop_angle = 0.125

AXES = ("tm", "site")
TIMES = 64
STRIPS = 4
HALF_ROWS = LY // 2
PAIRS = HALF_ROWS // 2
CORE_GROUPS = [
    [t * STRIPS + 2 * half + core for t in range(TIMES) for half in range(2)] for core in range(2)
]
CORE_SWAP = [(i, i ^ 1) for i in range(TIMES * STRIPS)]
VMEM_LIMIT = 50 * 1024 * 1024


def pack_kernel(initial_ref, fields_ref, out_ref):
    sign = jnp.where(lax.axis_index("tm") == 0, 1.0, -1.0).astype(jnp.float32)
    for q in range(8):
        rows = [
            initial_ref[pl.ds((2 * q + y) * LX + x, 8, stride=8), :]
            for y in range(2)
            for x in range(8)
        ]
        out_ref[pl.ds(q, PANEL, stride=16), :] = jnp.concatenate(rows, axis=0).T
        spin = fields_ref[:, q * 128 : (q + 1) * 128].astype(jnp.float32)
        growth = sign * jnp.exp(coupling * (2.0 * spin - 1.0))
        out_ref[pl.ds(8 + q, PANEL, stride=16), :] = jnp.broadcast_to(growth, (PANEL, 128))


def tables_kernel(bonds_ref, cos_ref, sin_ref, flat_ref):
    cos_less = math.cosh(hop_angle) - 1.0
    sin_full = math.sinh(hop_angle)
    upper = lax.broadcasted_iota(jnp.int32, (128, 128), 0) % 2 == 1
    for f in range(4):
        for q in range(8):
            low = bonds_ref[f : f + 1, q * 128 : (q + 1) * 128].astype(jnp.float32)
            high = bonds_ref[f : f + 1, 1024 + q * 128 : 1024 + (q + 1) * 128].astype(jnp.float32)
            both = jnp.where(
                upper, jnp.broadcast_to(high, (128, 128)), jnp.broadcast_to(low, (128, 128))
            )
            flat_ref[pl.ds(q * 128, 128), :] = both.T
        width = 4 if f < 2 else 8
        for i in range(128):
            start = (i // width) * width * 8 + i % width
            kept = flat_ref[pl.ds(start, 8, stride=width), :]
            cos_ref[f, i] = 1.0 + kept * cos_less
            sin_ref[f, i] = kept * sin_full


def rotate(former, latter, cos, sin):
    return cos * former + sin * latter, sin * former + cos * latter


def swap_halves(value, odd):
    return jnp.where(odd, pltpu.roll(value, 1, 1), pltpu.roll(value, 127, 1))


def solve_kernel(
    sites_ref, own_ref, other_ref, cos_ref, sin_ref, out_ref,
    flat, growth, direction, residual, image, answer, gradient, edge,
):
    core = lax.axis_index("site") % 2
    column = 2 * lax.axis_index("tm") + lax.axis_index("site") // 2
    odd = lax.broadcasted_iota(jnp.int32, (8, 128), 1) % 2 == 1

    for source_ref, place in ((own_ref, core), (other_ref, 1 - core)):
        for q in range(8):
            block = source_ref[pl.ds(q, PANEL, stride=16), :].T
            direction[pl.ds(place * 16 + 2 * q, 2)] = block.reshape(2, 8, 8, 128)
            block = source_ref[pl.ds(8 + q, PANEL, stride=16), :].T
            flat[pl.ds(place * 1024 + q * 128, 128), :] = block
    zero = jnp.zeros((8, 128), jnp.float32)
    for y in range(HALF_ROWS):
        for x in range(8):
            growth[y, x] = flat[pl.ds(y * LX + x, 8, stride=8), :]
            residual[y, x] = zero
            answer[y, x] = zero
            gradient[y, x] = zero

    site = sites_ref[column]
    source_lane = 2 * (column * SLICES // PANEL) + site // (HALF_ROWS * LX)
    source_x = site % LX
    here = (lax.broadcasted_iota(jnp.int32, (8, 128), 0) == source_x // 8) & (
        lax.broadcasted_iota(jnp.int32, (8, 128), 1) == source_lane
    )
    residual[(site // LX) % HALF_ROWS, source_x % 8] = jnp.where(here, 1.0, 0.0)

    def along_x(row, y):
        row = list(row)
        for j in range(4):
            i = y * 4 + j
            row[2 * j], row[2 * j + 1] = rotate(
                row[2 * j], row[2 * j + 1], cos_ref[0, i], sin_ref[0, i]
            )
        return row

    def along_x_shifted(row, y):
        row = list(row)
        for j in range(4):
            i = y * 4 + j
            cos, sin = cos_ref[1, i], sin_ref[1, i]
            if j < 3:
                row[2 * j + 1], row[2 * j + 2] = rotate(row[2 * j + 1], row[2 * j + 2], cos, sin)
            else:
                row[7], wrapped = rotate(row[7], pltpu.roll(row[0], 7, 0), cos, sin)
                row[0] = pltpu.roll(wrapped, 1, 0)
        return row

    def across(former, latter, family, pair):
        results = [
            rotate(former[x], latter[x], cos_ref[family, pair * 8 + x], sin_ref[family, pair * 8 + x])
            for x in range(8)
        ]
        return [r[0] for r in results], [r[1] for r in results]

    def across_halves(last, first):
        moved = [swap_halves(v, odd) for v in first]
        last, moved = across(last, moved, 3, PAIRS - 1)
        return last, [swap_halves(v, odd) for v in moved]

    def forward_pass(beta):
        def hopped(p):
            rows = []
            for y in (2 * p, 2 * p + 1):
                row = []
                for x in range(8):
                    value = gradient[y, x] + beta * direction[y, x]
                    direction[y, x] = value
                    row.append(pltpu.roll(value, 2, 1) * growth[y, x])
                rows.append(along_x_shifted(along_x(row, y), y))
            return across(rows[0], rows[1], 2, p)

        def put(row, y, total):
            for x in range(8):
                value = direction[y, x] + row[x]
                image[y, x] = value
                total = total + value * value
            return total

        first, last = hopped(0)
        for x in range(8):
            edge[x] = first[x]

        def step(p, carry):
            last, total = carry
            upper, lower = hopped(p)
            last, upper = across(last, upper, 3, p - 1)
            total = put(last, 2 * p - 1, total)
            total = put(upper, 2 * p, total)
            return lower, total

        last, total = lax.fori_loop(1, PAIRS, step, (last, zero))
        last, first = across_halves(last, [edge[x] for x in range(8)])
        total = put(last, HALF_ROWS - 1, total)
        total = put(first, 0, total)
        return jnp.sum(total, keepdims=True)

    def backward_pass(size):
        def updated(y):
            row = []
            for x in range(8):
                answer[y, x] = answer[y, x] + size * direction[y, x]
                value = residual[y, x] - size * image[y, x]
                residual[y, x] = value
                row.append(value)
            return row

        def finish(upper, lower, p, total):
            rows = across(upper, lower, 2, p)
            for row, y in zip(rows, (2 * p, 2 * p + 1)):
                row = along_x(along_x_shifted(row, y), y)
                for x in range(8):
                    value = residual[y, x] + pltpu.roll(row[x] * growth[y, x], 126, 1)
                    gradient[y, x] = value
                    total = total + value * value
            return total

        last, first = across_halves(updated(HALF_ROWS - 1), updated(0))
        for x in range(8):
            edge[x] = last[x]

        def step(p, carry):
            upper, total = carry
            lower, later = across(updated(2 * p + 1), updated(2 * p + 2), 3, p)
            total = finish(upper, lower, p, total)
            return later, total

        upper, total = lax.fori_loop(0, PAIRS - 1, step, (first, zero))
        total = finish(upper, [edge[x] for x in range(8)], PAIRS - 1, total)
        return jnp.sum(total, keepdims=True)

    def turn(k, carry):
        gamma, beta = carry
        squares = forward_pass(beta)
        size = jnp.where(k == 0, jnp.ones_like(gamma), gamma / squares)
        gamma_next = backward_pass(size)
        beta = jnp.where(k == 0, jnp.zeros_like(gamma), gamma_next / gamma)
        return gamma_next, beta

    one = jnp.ones((1, 1), jnp.float32)
    lax.fori_loop(0, ITERS + 1, turn, (one, one))

    for part, values in enumerate((answer, gradient)):
        for q in range(8):
            block = values[pl.ds(core * 16 + 2 * q, 2)].reshape(128, 128)
            out_ref[pl.ds(8 * part + q, PANEL, stride=16), :] = block.T


def unpack_kernel(arrived_ref, solution_ref, gradient_ref):
    for part, out_ref in enumerate((solution_ref, gradient_ref)):
        for q in range(8):
            block = arrived_ref[pl.ds(8 * part + q, PANEL, stride=16), :].T
            for y in range(2):
                for x in range(8):
                    i = y * 8 + x
                    out_ref[pl.ds((2 * q + y) * LX + x, 8, stride=8), :] = block[8 * i : 8 * i + 8]


def call(kernel, out_shape, scratch=(), smem_first=False, operands=1, cost=0):
    vmem = pl.BlockSpec(memory_space=pltpu.VMEM)
    in_specs = [vmem] * operands
    if smem_first:
        in_specs[0] = pl.BlockSpec(memory_space=pltpu.SMEM)
    return pl.pallas_call(
        kernel,
        out_shape=out_shape,
        in_specs=in_specs,
        out_specs=jax.tree.map(lambda _: vmem, out_shape),
        scratch_shapes=list(scratch),
        compiler_params=pltpu.CompilerParams(vmem_limit_bytes=VMEM_LIMIT),
        cost_estimate=pl.CostEstimate(flops=cost, bytes_accessed=1 << 20, transcendentals=0),
    )


def f32(*shape):
    return jax.ShapeDtypeStruct(shape, jnp.float32)


def exchange(values):
    parts = values.reshape(PANEL, 16, 128)
    moved = lax.all_to_all(parts, AXES, 0, 0, tiled=True, axis_index_groups=CORE_GROUPS)
    return moved.reshape(PANEL * 16, 128)


def body(fields, bonds, source_sites, initial):
    packed = call(pack_kernel, f32(PANEL * 16, 128), operands=2)(
        initial.reshape(1024, PANEL), fields
    )
    cos, sin = call(
        tables_kernel,
        (f32(4, 128, 8, 128), f32(4, 128, 8, 128)),
        scratch=[pltpu.VMEM((1024, 128), jnp.float32)],
        cost=10_000_000,
    )(bonds)
    own = exchange(packed)
    other = lax.ppermute(own, AXES, CORE_SWAP)
    lattice = pltpu.VMEM((HALF_ROWS, 8, 8, 128), jnp.float32)
    solved = call(
        solve_kernel,
        f32(PANEL * 16, 128),
        scratch=[pltpu.VMEM((2048, 128), jnp.float32)]
        + [lattice] * 6
        + [pltpu.VMEM((8, 8, 128), jnp.float32)],
        smem_first=True,
        operands=5,
    )(source_sites, own, other, cos, sin)
    arrived = exchange(solved)
    solution, gradient = call(unpack_kernel, (f32(1024, PANEL), f32(1024, PANEL)))(arrived)
    return solution.reshape(1, 1024, PANEL), gradient.reshape(1, 1024, PANEL)


def solution(mesh):
    placed = (P("tm", "site"), P(), P(), P("tm", "site", None))
    return jax.shard_map(
        body,
        mesh=mesh,
        in_specs=placed,
        out_specs=(P("tm", "site", None), P("tm", "site", None)),
        check_vma=False,
    )
```

```python
import math

import jax
import jax.numpy as jnp
from jax import lax
from jax.experimental import pallas as pl
from jax.experimental.pallas import tpu as pltpu
from jax.sharding import PartitionSpec as P

LX = 64
LY = 64
PANEL = 128
SLICES = 64
ITERS = 6

coupling = 0.7368
hop_angle = 0.125

AXES = ("tm", "site")
TIMES = 64
STRIPS = 4
HALF_ROWS = LY // 2
PAIRS = HALF_ROWS // 2
CORE_GROUPS = [
    [t * STRIPS + 2 * half + core for t in range(TIMES) for half in range(2)] for core in range(2)
]
CORE_SWAP = [(i, i ^ 1) for i in range(TIMES * STRIPS)]
VMEM_LIMIT = 50 * 1024 * 1024


def pack_kernel(initial_ref, fields_ref, out_ref):
    sign = jnp.where(lax.axis_index("tm") == 0, 1.0, -1.0).astype(jnp.float32)
    for q in range(8):
        rows = [
            initial_ref[pl.ds((2 * q + y) * LX + x, 8, stride=8), :]
            for y in range(2)
            for x in range(8)
        ]
        out_ref[pl.ds(q, PANEL, stride=16), :] = jnp.concatenate(rows, axis=0).T
        spin = fields_ref[:, q * 128 : (q + 1) * 128].astype(jnp.float32)
        growth = sign * jnp.exp(coupling * (2.0 * spin - 1.0))
        out_ref[pl.ds(8 + q, PANEL, stride=16), :] = jnp.broadcast_to(growth, (PANEL, 128))


def tables_kernel(bonds_ref, cos_ref, sin_ref, flat_ref):
    cos_less = math.cosh(hop_angle) - 1.0
    sin_full = math.sinh(hop_angle)
    upper = lax.broadcasted_iota(jnp.int32, (128, 128), 0) % 2 == 1
    for f in range(4):
        for q in range(8):
            low = bonds_ref[f : f + 1, q * 128 : (q + 1) * 128].astype(jnp.float32)
            high = bonds_ref[f : f + 1, 1024 + q * 128 : 1024 + (q + 1) * 128].astype(jnp.float32)
            both = jnp.where(
                upper, jnp.broadcast_to(high, (128, 128)), jnp.broadcast_to(low, (128, 128))
            )
            flat_ref[pl.ds(q * 128, 128), :] = both.T
        width = 4 if f < 2 else 8
        for i in range(128):
            start = (i // width) * width * 8 + i % width
            kept = flat_ref[pl.ds(start, 8, stride=width), :]
            cos_ref[f, i] = 1.0 + kept * cos_less
            sin_ref[f, i] = kept * sin_full


def rotate(former, latter, cos, sin):
    return cos * former + sin * latter, sin * former + cos * latter


def swap_halves(value, odd):
    return jnp.where(odd, pltpu.roll(value, 1, 1), pltpu.roll(value, 127, 1))


def solve_kernel(
    sites_ref, own_ref, other_ref, cos_ref, sin_ref, out_ref,
    flat, growth, direction, residual, image, answer, gradient, edge,
):
    core = lax.axis_index("site") % 2
    column = 2 * lax.axis_index("tm") + lax.axis_index("site") // 2
    odd = lax.broadcasted_iota(jnp.int32, (8, 128), 1) % 2 == 1

    for source_ref, place in ((own_ref, core), (other_ref, 1 - core)):
        for q in range(8):
            block = source_ref[pl.ds(q, PANEL, stride=16), :].T
            direction[pl.ds(place * 16 + 2 * q, 2)] = block.reshape(2, 8, 8, 128)
            block = source_ref[pl.ds(8 + q, PANEL, stride=16), :].T
            flat[pl.ds(place * 1024 + q * 128, 128), :] = block
    zero = jnp.zeros((8, 128), jnp.float32)
    for y in range(HALF_ROWS):
        for x in range(8):
            growth[y, x] = flat[pl.ds(y * LX + x, 8, stride=8), :]
            residual[y, x] = zero
            answer[y, x] = zero
            gradient[y, x] = zero

    site = sites_ref[column]
    source_lane = 2 * (column * SLICES // PANEL) + site // (HALF_ROWS * LX)
    source_x = site % LX
    here = (lax.broadcasted_iota(jnp.int32, (8, 128), 0) == source_x // 8) & (
        lax.broadcasted_iota(jnp.int32, (8, 128), 1) == source_lane
    )
    residual[(site // LX) % HALF_ROWS, source_x % 8] = jnp.where(here, 1.0, 0.0)

    def along_x(row, y):
        row = list(row)
        for j in range(4):
            i = y * 4 + j
            row[2 * j], row[2 * j + 1] = rotate(
                row[2 * j], row[2 * j + 1], cos_ref[0, i], sin_ref[0, i]
            )
        return row

    def along_x_shifted(row, y):
        row = list(row)
        for j in range(4):
            i = y * 4 + j
            cos, sin = cos_ref[1, i], sin_ref[1, i]
            if j < 3:
                row[2 * j + 1], row[2 * j + 2] = rotate(row[2 * j + 1], row[2 * j + 2], cos, sin)
            else:
                row[7], wrapped = rotate(row[7], pltpu.roll(row[0], 7, 0), cos, sin)
                row[0] = pltpu.roll(wrapped, 1, 0)
        return row

    def across(former, latter, family, pair):
        results = [
            rotate(former[x], latter[x], cos_ref[family, pair * 8 + x], sin_ref[family, pair * 8 + x])
            for x in range(8)
        ]
        return [r[0] for r in results], [r[1] for r in results]

    def across_halves(last, first):
        moved = [swap_halves(v, odd) for v in first]
        last, moved = across(last, moved, 3, PAIRS - 1)
        return last, [swap_halves(v, odd) for v in moved]

    def forward_pass(beta):
        def hopped(p):
            rows = []
            for y in (2 * p, 2 * p + 1):
                row = []
                for x in range(8):
                    value = gradient[y, x] + beta * direction[y, x]
                    direction[y, x] = value
                    row.append(pltpu.roll(value, 2, 1) * growth[y, x])
                rows.append(along_x_shifted(along_x(row, y), y))
            return across(rows[0], rows[1], 2, p)

        def put(row, y, total):
            for x in range(8):
                value = direction[y, x] + row[x]
                image[y, x] = value
                total = total + value * value
            return total

        first, last = hopped(0)
        for x in range(8):
            edge[x] = first[x]

        def step(p, carry):
            last, total = carry
            upper, lower = hopped(p)
            last, upper = across(last, upper, 3, p - 1)
            total = put(last, 2 * p - 1, total)
            total = put(upper, 2 * p, total)
            return lower, total

        carry = (last, zero)
        for p in range(1, PAIRS):
            carry = step(p, carry)
        last, total = carry
        last, first = across_halves(last, [edge[x] for x in range(8)])
        total = put(last, HALF_ROWS - 1, total)
        total = put(first, 0, total)
        return jnp.sum(total, keepdims=True)

    def backward_pass(size):
        def updated(y):
            row = []
            for x in range(8):
                answer[y, x] = answer[y, x] + size * direction[y, x]
                value = residual[y, x] - size * image[y, x]
                residual[y, x] = value
                row.append(value)
            return row

        def finish(upper, lower, p, total):
            rows = across(upper, lower, 2, p)
            for row, y in zip(rows, (2 * p, 2 * p + 1)):
                row = along_x(along_x_shifted(row, y), y)
                for x in range(8):
                    value = residual[y, x] + pltpu.roll(row[x] * growth[y, x], 126, 1)
                    gradient[y, x] = value
                    total = total + value * value
            return total

        last, first = across_halves(updated(HALF_ROWS - 1), updated(0))
        for x in range(8):
            edge[x] = last[x]

        def step(p, carry):
            upper, total = carry
            lower, later = across(updated(2 * p + 1), updated(2 * p + 2), 3, p)
            total = finish(upper, lower, p, total)
            return later, total

        carry = (first, zero)
        for p in range(PAIRS - 1):
            carry = step(p, carry)
        upper, total = carry
        total = finish(upper, [edge[x] for x in range(8)], PAIRS - 1, total)
        return jnp.sum(total, keepdims=True)

    def turn(k, carry):
        gamma, beta = carry
        squares = forward_pass(beta)
        size = jnp.where(k == 0, jnp.ones_like(gamma), gamma / squares)
        gamma_next = backward_pass(size)
        beta = jnp.where(k == 0, jnp.zeros_like(gamma), gamma_next / gamma)
        return gamma_next, beta

    one = jnp.ones((1, 1), jnp.float32)
    lax.fori_loop(0, ITERS + 1, turn, (one, one))

    for part, values in enumerate((answer, gradient)):
        for q in range(8):
            block = values[pl.ds(core * 16 + 2 * q, 2)].reshape(128, 128)
            out_ref[pl.ds(8 * part + q, PANEL, stride=16), :] = block.T


def unpack_kernel(arrived_ref, solution_ref, gradient_ref):
    for part, out_ref in enumerate((solution_ref, gradient_ref)):
        for q in range(8):
            block = arrived_ref[pl.ds(8 * part + q, PANEL, stride=16), :].T
            for y in range(2):
                for x in range(8):
                    i = y * 8 + x
                    out_ref[pl.ds((2 * q + y) * LX + x, 8, stride=8), :] = block[8 * i : 8 * i + 8]


def call(kernel, out_shape, scratch=(), smem_first=False, operands=1, cost=0):
    vmem = pl.BlockSpec(memory_space=pltpu.VMEM)
    in_specs = [vmem] * operands
    if smem_first:
        in_specs[0] = pl.BlockSpec(memory_space=pltpu.SMEM)
    return pl.pallas_call(
        kernel,
        out_shape=out_shape,
        in_specs=in_specs,
        out_specs=jax.tree.map(lambda _: vmem, out_shape),
        scratch_shapes=list(scratch),
        compiler_params=pltpu.CompilerParams(vmem_limit_bytes=VMEM_LIMIT),
        cost_estimate=pl.CostEstimate(flops=cost, bytes_accessed=1 << 20, transcendentals=0),
    )


def f32(*shape):
    return jax.ShapeDtypeStruct(shape, jnp.float32)


def exchange(values):
    parts = values.reshape(PANEL, 16, 128)
    moved = lax.all_to_all(parts, AXES, 0, 0, tiled=True, axis_index_groups=CORE_GROUPS)
    return moved.reshape(PANEL * 16, 128)


def local_solve(source_sites, own, other, bonds):
    cos, sin = call(
        tables_kernel,
        (f32(4, 128, 8, 128), f32(4, 128, 8, 128)),
        scratch=[pltpu.VMEM((1024, 128), jnp.float32)],
        cost=10_000_000,
    )(bonds)
    lattice = pltpu.VMEM((HALF_ROWS, 8, 8, 128), jnp.float32)
    return call(
        solve_kernel,
        f32(PANEL * 16, 128),
        scratch=[pltpu.VMEM((2048, 128), jnp.float32)]
        + [lattice] * 6
        + [pltpu.VMEM((8, 8, 128), jnp.float32)],
        smem_first=True,
        operands=5,
    )(source_sites, own, other, cos, sin)


def body(fields, bonds, source_sites, initial):
    packed = call(pack_kernel, f32(PANEL * 16, 128), operands=2)(
        initial.reshape(1024, PANEL), fields
    )
    own = exchange(packed)
    other = lax.ppermute(own, AXES, CORE_SWAP)
    solved = local_solve(source_sites, own, other, bonds)
    arrived = exchange(solved)
    solution, gradient = call(unpack_kernel, (f32(1024, PANEL), f32(1024, PANEL)))(arrived)
    return solution.reshape(1, 1024, PANEL), gradient.reshape(1, 1024, PANEL)


def solution(mesh):
    placed = (P("tm", "site"), P(), P(), P("tm", "site", None))
    return jax.shard_map(
        body,
        mesh=mesh,
        in_specs=placed,
        out_specs=(P("tm", "site", None), P("tm", "site", None)),
        check_vma=False,
    )
```

```python
import math

import jax
import jax.numpy as jnp
from jax import lax
from jax.experimental import pallas as pl
from jax.experimental.pallas import tpu as pltpu
from jax.sharding import PartitionSpec as P

LX = 64
LY = 64
PANEL = 128
SLICES = 64
ITERS = 6

coupling = 0.7368
hop_angle = 0.125

AXES = ("tm", "site")
TIMES = 64
STRIPS = 4
HALF_ROWS = LY // 2
PAIRS = HALF_ROWS // 2
CORE_GROUPS = [
    [t * STRIPS + 2 * half + core for t in range(TIMES) for half in range(2)] for core in range(2)
]
CORE_SWAP = [(i, i ^ 1) for i in range(TIMES * STRIPS)]
UNROLL = 15
VMEM_LIMIT = 50 * 1024 * 1024


def pack_kernel(initial_ref, fields_ref, out_ref):
    sign = jnp.where(lax.axis_index("tm") == 0, 1.0, -1.0).astype(jnp.float32)
    for q in range(8):
        rows = [
            initial_ref[pl.ds((2 * q + y) * LX + x, 8, stride=8), :]
            for y in range(2)
            for x in range(8)
        ]
        out_ref[pl.ds(q, PANEL, stride=16), :] = jnp.concatenate(rows, axis=0).T
        spin = fields_ref[:, q * 128 : (q + 1) * 128].astype(jnp.float32)
        growth = sign * jnp.exp(coupling * (2.0 * spin - 1.0))
        out_ref[pl.ds(8 + q, PANEL, stride=16), :] = jnp.broadcast_to(growth, (PANEL, 128))


def tables_kernel(bonds_ref, tan_ref, mix_ref, flat_ref, cos_ref):
    cos_less = math.cosh(hop_angle) - 1.0
    tangent = math.tanh(hop_angle)
    odd = lax.broadcasted_iota(jnp.int32, (8, 128), 1) % 2 == 1
    upper = lax.broadcasted_iota(jnp.int32, (128, 128), 0) % 2 == 1
    for f in range(4):
        for q in range(8):
            low = bonds_ref[f : f + 1, q * 128 : (q + 1) * 128].astype(jnp.float32)
            high = bonds_ref[f : f + 1, 1024 + q * 128 : 1024 + (q + 1) * 128].astype(jnp.float32)
            both = jnp.where(
                upper, jnp.broadcast_to(high, (128, 128)), jnp.broadcast_to(low, (128, 128))
            )
            flat_ref[f, pl.ds(q * 128, 128), :] = both.T
        if f == 2:
            continue
        width = 4 if f < 2 else 8
        for i in range(128):
            start = (i // width) * width * 8 + i % width
            kept = flat_ref[f, pl.ds(start, 8, stride=width), :]
            tan_ref[f - f // 3, i] = kept * tangent
            if f > 0:
                cos_ref[f // 3, i] = 1.0 + kept * cos_less

    def cos_along(y, x):
        if x == 0:
            return pltpu.roll(cos_ref[0, y * 4 + 3], 1, 0)
        return cos_ref[0, y * 4 + (x - 1) // 2]

    for p in range(PAIRS):
        for x in range(8):
            kept = flat_ref[2, pl.ds(p * 64 + x, 8, stride=8), :]
            cos, sin = 1.0 + kept * cos_less, kept * math.sinh(hop_angle)
            if p == 0:
                before = swap_halves(cos_ref[1, (PAIRS - 1) * 8 + x], odd)
            else:
                before = cos_ref[1, (p - 1) * 8 + x]
            after = cos_ref[1, p * 8 + x]
            former, latter = cos_along(2 * p, x), cos_along(2 * p + 1, x)
            mix_ref[0, p * 8 + x] = before * cos * former
            mix_ref[1, p * 8 + x] = before * sin * latter
            mix_ref[2, p * 8 + x] = after * sin * former
            mix_ref[3, p * 8 + x] = after * cos * latter


def join(former, latter, tan):
    return former + tan * latter, latter + tan * former


def swap_halves(value, odd):
    return jnp.where(odd, pltpu.roll(value, 1, 1), pltpu.roll(value, 127, 1))


def solve_kernel(
    sites_ref, own_ref, other_ref, tan_ref, mix_ref, out_ref,
    flat, growth, direction, residual, image, answer, gradient, edge,
):
    core = lax.axis_index("site") % 2
    column = 2 * lax.axis_index("tm") + lax.axis_index("site") // 2
    odd = lax.broadcasted_iota(jnp.int32, (8, 128), 1) % 2 == 1

    for source_ref, place in ((own_ref, core), (other_ref, 1 - core)):
        for q in range(8):
            block = source_ref[pl.ds(q, PANEL, stride=16), :].T
            direction[pl.ds(place * 16 + 2 * q, 2)] = block.reshape(2, 8, 8, 128)
            block = source_ref[pl.ds(8 + q, PANEL, stride=16), :].T
            flat[pl.ds(place * 1024 + q * 128, 128), :] = block
    zero = jnp.zeros((8, 128), jnp.float32)
    for y in range(HALF_ROWS):
        for x in range(8):
            cos = jnp.where(tan_ref[0, y * 4 + x // 2] > 0.0, math.cosh(hop_angle), 1.0)
            growth[y, x] = flat[pl.ds(y * LX + x, 8, stride=8), :] * cos
            residual[y, x] = zero
            answer[y, x] = zero
            gradient[y, x] = zero

    site = sites_ref[column]
    source_lane = 2 * (column * SLICES // PANEL) + site // (HALF_ROWS * LX)
    source_x = site % LX
    here = (lax.broadcasted_iota(jnp.int32, (8, 128), 0) == source_x // 8) & (
        lax.broadcasted_iota(jnp.int32, (8, 128), 1) == source_lane
    )
    residual[(site // LX) % HALF_ROWS, source_x % 8] = jnp.where(here, 1.0, 0.0)

    def along_x(row, y):
        row = list(row)
        for j in range(4):
            row[2 * j], row[2 * j + 1] = join(row[2 * j], row[2 * j + 1], tan_ref[0, y * 4 + j])
        return row

    def along_x_shifted(row, y):
        row = list(row)
        for j in range(3):
            row[2 * j + 1], row[2 * j + 2] = join(
                row[2 * j + 1], row[2 * j + 2], tan_ref[1, y * 4 + j]
            )
        row[7], wrapped = join(row[7], pltpu.roll(row[0], 7, 0), tan_ref[1, y * 4 + 3])
        row[0] = pltpu.roll(wrapped, 1, 0)
        return row

    def mixed(former, latter, pair, order):
        results = [[], []]
        for x in range(8):
            i = pair * 8 + x
            for side, (m, n) in enumerate(order):
                results[side].append(mix_ref[m, i] * former[x] + mix_ref[n, i] * latter[x])
        return results

    def across(former, latter, pair):
        results = [join(former[x], latter[x], tan_ref[2, pair * 8 + x]) for x in range(8)]
        return [r[0] for r in results], [r[1] for r in results]

    def across_halves(last, first):
        moved = [swap_halves(v, odd) for v in first]
        last, moved = across(last, moved, PAIRS - 1)
        return last, [swap_halves(v, odd) for v in moved]

    def add_squares(totals, x, value):
        totals = list(totals)
        totals[x % 4] = totals[x % 4] + value * value
        return totals

    def loop(first, steps, step, carry):
        if steps % UNROLL:
            raise ValueError("bad unroll")

        def turn(i, carry):
            for j in range(UNROLL):
                carry = step(first + i * UNROLL + j, carry)
            return carry

        if steps == UNROLL:
            return turn(0, carry)
        return lax.fori_loop(0, steps // UNROLL, turn, carry)

    def forward_pass(beta):
        def hopped(p):
            rows = []
            for y in (2 * p, 2 * p + 1):
                row = []
                for x in range(8):
                    value = gradient[y, x] + beta * direction[y, x]
                    direction[y, x] = value
                    row.append(pltpu.roll(value, 2, 1) * growth[y, x])
                rows.append(along_x_shifted(along_x(row, y), y))
            return mixed(rows[0], rows[1], p, ((0, 1), (2, 3)))

        def put(row, y, totals):
            for x in range(8):
                value = direction[y, x] + row[x]
                image[y, x] = value
                totals = add_squares(totals, x, value)
            return totals

        first, last = hopped(0)
        for x in range(8):
            edge[x] = first[x]

        def step(p, carry):
            last, totals = carry
            upper, lower = hopped(p)
            last, upper = across(last, upper, p - 1)
            totals = put(last, 2 * p - 1, totals)
            totals = put(upper, 2 * p, totals)
            return lower, totals

        last, totals = loop(1, PAIRS - 1, step, (last, [zero] * 4))
        last, first = across_halves(last, [edge[x] for x in range(8)])
        totals = put(last, HALF_ROWS - 1, totals)
        totals = put(first, 0, totals)
        return jnp.sum(sum(totals), keepdims=True)

    def backward_pass(size):
        def updated(y):
            row = []
            for x in range(8):
                answer[y, x] = answer[y, x] + size * direction[y, x]
                value = residual[y, x] - size * image[y, x]
                residual[y, x] = value
                row.append(value)
            return row

        def finish(upper, lower, p, totals):
            rows = mixed(upper, lower, p, ((0, 2), (1, 3)))
            for row, y in zip(rows, (2 * p, 2 * p + 1)):
                row = along_x(along_x_shifted(row, y), y)
                for x in range(8):
                    value = residual[y, x] + pltpu.roll(row[x] * growth[y, x], 126, 1)
                    gradient[y, x] = value
                    totals = add_squares(totals, x, value)
            return totals

        last, first = across_halves(updated(HALF_ROWS - 1), updated(0))
        for x in range(8):
            edge[x] = last[x]

        def step(p, carry):
            upper, totals = carry
            lower, later = across(updated(2 * p + 1), updated(2 * p + 2), p)
            totals = finish(upper, lower, p, totals)
            return later, totals

        upper, totals = loop(0, PAIRS - 1, step, (first, [zero] * 4))
        totals = finish(upper, [edge[x] for x in range(8)], PAIRS - 1, totals)
        return jnp.sum(sum(totals), keepdims=True)

    def turn(k, carry):
        gamma, beta = carry
        squares = forward_pass(beta)
        size = jnp.where(k == 0, jnp.ones_like(gamma), gamma / squares)
        gamma_next = backward_pass(size)
        beta = jnp.where(k == 0, jnp.zeros_like(gamma), gamma_next / gamma)
        return gamma_next, beta

    one = jnp.ones((1, 1), jnp.float32)
    lax.fori_loop(0, ITERS + 1, turn, (one, one))

    for part, values in enumerate((answer, gradient)):
        for q in range(8):
            block = values[pl.ds(core * 16 + 2 * q, 2)].reshape(128, 128)
            out_ref[pl.ds(8 * part + q, PANEL, stride=16), :] = block.T


def unpack_kernel(arrived_ref, solution_ref, gradient_ref):
    for part, out_ref in enumerate((solution_ref, gradient_ref)):
        for q in range(8):
            block = arrived_ref[pl.ds(8 * part + q, PANEL, stride=16), :].T
            for y in range(2):
                for x in range(8):
                    i = y * 8 + x
                    out_ref[pl.ds((2 * q + y) * LX + x, 8, stride=8), :] = block[8 * i : 8 * i + 8]


def call(kernel, out_shape, scratch=(), smem_first=False, operands=1, cost=0):
    vmem = pl.BlockSpec(memory_space=pltpu.VMEM)
    in_specs = [vmem] * operands
    if smem_first:
        in_specs[0] = pl.BlockSpec(memory_space=pltpu.SMEM)
    return pl.pallas_call(
        kernel,
        out_shape=out_shape,
        in_specs=in_specs,
        out_specs=jax.tree.map(lambda _: vmem, out_shape),
        scratch_shapes=list(scratch),
        compiler_params=pltpu.CompilerParams(vmem_limit_bytes=VMEM_LIMIT),
        cost_estimate=pl.CostEstimate(flops=cost, bytes_accessed=1 << 20, transcendentals=0),
    )


def f32(*shape):
    return jax.ShapeDtypeStruct(shape, jnp.float32)


def exchange(values):
    parts = values.reshape(PANEL, 16, 128)
    moved = lax.all_to_all(parts, AXES, 0, 0, tiled=True, axis_index_groups=CORE_GROUPS)
    return moved.reshape(PANEL * 16, 128)


def local_solve(source_sites, own, other, bonds):
    tan, mix = call(
        tables_kernel,
        (f32(3, 128, 8, 128), f32(4, 128, 8, 128)),
        scratch=[
            pltpu.VMEM((4, 1024, 128), jnp.float32),
            pltpu.VMEM((2, 128, 8, 128), jnp.float32),
        ],
        cost=10_000_000,
    )(bonds)
    lattice = pltpu.VMEM((HALF_ROWS, 8, 8, 128), jnp.float32)
    return call(
        solve_kernel,
        f32(PANEL * 16, 128),
        scratch=[pltpu.VMEM((2048, 128), jnp.float32)]
        + [lattice] * 6
        + [pltpu.VMEM((8, 8, 128), jnp.float32)],
        smem_first=True,
        operands=5,
    )(source_sites, own, other, tan, mix)


def body(fields, bonds, source_sites, initial):
    packed = call(pack_kernel, f32(PANEL * 16, 128), operands=2)(
        initial.reshape(1024, PANEL), fields
    )
    own = exchange(packed)
    other = lax.ppermute(own, AXES, CORE_SWAP)
    solved = local_solve(source_sites, own, other, bonds)
    arrived = exchange(solved)
    solution, gradient = call(unpack_kernel, (f32(1024, PANEL), f32(1024, PANEL)))(arrived)
    return solution.reshape(1, 1024, PANEL), gradient.reshape(1, 1024, PANEL)


def solution(mesh):
    placed = (P("tm", "site"), P(), P(), P("tm", "site", None))
    return jax.shard_map(
        body,
        mesh=mesh,
        in_specs=placed,
        out_specs=(P("tm", "site", None), P("tm", "site", None)),
        check_vma=False,
    )
```

```python
import math

import jax
import jax.numpy as jnp
from jax import lax
from jax.experimental import pallas as pl
from jax.experimental.pallas import tpu as pltpu
from jax.sharding import PartitionSpec as P

LX = 64
LY = 64
PANEL = 128
SLICES = 64
ITERS = 6

coupling = 0.7368
hop_angle = 0.125

AXES = ("tm", "site")
TIMES = 64
STRIPS = 4
HALF_ROWS = LY // 2
PAIRS = HALF_ROWS // 2
CORE_GROUPS = [
    [t * STRIPS + 2 * half + core for t in range(TIMES) for half in range(2)] for core in range(2)
]
CORE_SWAP = [(i, i ^ 1) for i in range(TIMES * STRIPS)]
VMEM_LIMIT = 24 * 1024 * 1024


def pack_kernel(initial_ref, fields_ref, out_ref):
    sign = jnp.where(lax.axis_index("tm") == 0, 1.0, -1.0).astype(jnp.float32)
    for q in range(8):
        rows = [
            initial_ref[pl.ds((2 * q + y) * LX + x, 8, stride=8), :]
            for y in range(2)
            for x in range(8)
        ]
        out_ref[pl.ds(q, PANEL, stride=16), :] = jnp.concatenate(rows, axis=0).T
        spin = fields_ref[:, q * 128 : (q + 1) * 128].astype(jnp.float32)
        growth = sign * jnp.exp(coupling * (2.0 * spin - 1.0))
        out_ref[pl.ds(8 + q, PANEL, stride=16), :] = jnp.broadcast_to(growth, (PANEL, 128))


def tables_kernel(bonds_ref, tan_ref, mix_ref, flat_ref, cos_ref):
    cos_less = math.cosh(hop_angle) - 1.0
    tangent = math.tanh(hop_angle)
    odd = lax.broadcasted_iota(jnp.int32, (8, 128), 1) % 2 == 1
    upper = lax.broadcasted_iota(jnp.int32, (128, 128), 0) % 2 == 1
    for f in range(4):
        for q in range(8):
            low = bonds_ref[f : f + 1, q * 128 : (q + 1) * 128].astype(jnp.float32)
            high = bonds_ref[f : f + 1, 1024 + q * 128 : 1024 + (q + 1) * 128].astype(jnp.float32)
            both = jnp.where(
                upper, jnp.broadcast_to(high, (128, 128)), jnp.broadcast_to(low, (128, 128))
            )
            flat_ref[f, pl.ds(q * 128, 128), :] = both.T
        if f == 2:
            continue
        width = 4 if f < 2 else 8
        for i in range(128):
            start = (i // width) * width * 8 + i % width
            kept = flat_ref[f, pl.ds(start, 8, stride=width), :]
            tan_ref[f - f // 3, i] = kept * tangent
            if f > 0:
                cos_ref[f // 3, i] = 1.0 + kept * cos_less

    def cos_along(y, x):
        if x == 0:
            return pltpu.roll(cos_ref[0, y * 4 + 3], 1, 0)
        return cos_ref[0, y * 4 + (x - 1) // 2]

    for p in range(PAIRS):
        for x in range(8):
            kept = flat_ref[2, pl.ds(p * 64 + x, 8, stride=8), :]
            cos, sin = 1.0 + kept * cos_less, kept * math.sinh(hop_angle)
            if p == 0:
                before = swap_halves(cos_ref[1, (PAIRS - 1) * 8 + x], odd)
            else:
                before = cos_ref[1, (p - 1) * 8 + x]
            after = cos_ref[1, p * 8 + x]
            former, latter = cos_along(2 * p, x), cos_along(2 * p + 1, x)
            mix_ref[0, p * 8 + x] = before * cos * former
            mix_ref[1, p * 8 + x] = before * sin * latter
            mix_ref[2, p * 8 + x] = after * sin * former
            mix_ref[3, p * 8 + x] = after * cos * latter


def join(former, latter, tan):
    return former + tan * latter, latter + tan * former


def swap_halves(value, odd):
    return jnp.where(odd, pltpu.roll(value, 1, 1), pltpu.roll(value, 127, 1))


def solve_kernel(
    sites_ref, own_ref, other_ref, tan_ref, mix_ref, out_ref,
    flat, growth, growth_before, gradient, history, image, edge, steps, betas,
):
    core = lax.axis_index("site") % 2
    column = 2 * lax.axis_index("tm") + lax.axis_index("site") // 2
    odd = lax.broadcasted_iota(jnp.int32, (8, 128), 1) % 2 == 1

    for source_ref, place in ((own_ref, core), (other_ref, 1 - core)):
        for q in range(8):
            block = source_ref[pl.ds(q, PANEL, stride=16), :].T
            gradient[pl.ds(place * 16 + 2 * q, 2)] = block.reshape(2, 8, 8, 128)
            block = source_ref[pl.ds(8 + q, PANEL, stride=16), :].T
            flat[pl.ds(place * 1024 + q * 128, 128), :] = block
    zero = jnp.zeros((8, 128), jnp.float32)
    for y in range(HALF_ROWS):
        for x in range(8):
            cos = jnp.where(tan_ref[0, y * 4 + x // 2] > 0.0, math.cosh(hop_angle), 1.0)
            value = flat[pl.ds(y * LX + x, 8, stride=8), :] * cos
            growth[y, x] = value
            growth_before[y, x] = pltpu.roll(value, 126, 1)
            image[y, x] = zero
            history[ITERS + 1, y, x] = zero

    site = sites_ref[column]
    source_lane = 2 * (column * SLICES // PANEL) + site // (HALF_ROWS * LX)
    source_x = site % LX
    here = (lax.broadcasted_iota(jnp.int32, (8, 128), 0) == source_x // 8) & (
        lax.broadcasted_iota(jnp.int32, (8, 128), 1) == source_lane
    )
    image[(site // LX) % HALF_ROWS, source_x % 8] = jnp.where(here, 1.0, 0.0)

    def along_x(row, y):
        row = list(row)
        for j in range(4):
            row[2 * j], row[2 * j + 1] = join(row[2 * j], row[2 * j + 1], tan_ref[0, y * 4 + j])
        return row

    def along_x_shifted(row, y):
        row = list(row)
        for j in range(3):
            row[2 * j + 1], row[2 * j + 2] = join(
                row[2 * j + 1], row[2 * j + 2], tan_ref[1, y * 4 + j]
            )
        row[7], wrapped = join(row[7], pltpu.roll(row[0], 7, 0), tan_ref[1, y * 4 + 3])
        row[0] = pltpu.roll(wrapped, 1, 0)
        return row

    def mixed(former, latter, pair, order):
        results = [[], []]
        for x in range(8):
            i = pair * 8 + x
            for side, (m, n) in enumerate(order):
                results[side].append(mix_ref[m, i] * former[x] + mix_ref[n, i] * latter[x])
        return results

    def across(former, latter, pair):
        results = [join(former[x], latter[x], tan_ref[2, pair * 8 + x]) for x in range(8)]
        return [r[0] for r in results], [r[1] for r in results]

    def across_halves(last, first):
        moved = [swap_halves(v, odd) for v in first]
        last, moved = across(last, moved, PAIRS - 1)
        return last, [swap_halves(v, odd) for v in moved]

    def add_squares(totals, x, value):
        totals = list(totals)
        totals[x % 4] = totals[x % 4] + value * value
        return totals

    def forward_pass(k, beta):
        def hopped(p):
            rows = []
            for y in (2 * p, 2 * p + 1):
                row = []
                for x in range(8):
                    value = gradient[y, x]
                    history[k, y, x] = value
                    row.append(value * growth_before[y, x])
                rows.append(along_x_shifted(along_x(row, y), y))
            return mixed(rows[0], rows[1], p, ((0, 1), (2, 3)))

        def put(row, y, totals):
            for x in range(8):
                value = (gradient[y, x] + pltpu.roll(row[x], 2, 1)) + beta * image[y, x]
                image[y, x] = value
                totals = add_squares(totals, x, value)
            return totals

        totals = [zero] * 4
        first, last = hopped(0)
        for x in range(8):
            edge[x] = first[x]
        for p in range(1, PAIRS):
            upper, lower = hopped(p)
            last, upper = across(last, upper, p - 1)
            totals = put(last, 2 * p - 1, totals)
            totals = put(upper, 2 * p, totals)
            last = lower
        last, first = across_halves(last, [edge[x] for x in range(8)])
        totals = put(last, HALF_ROWS - 1, totals)
        return put(first, 0, totals)

    def backward_pass(base, size):
        def loaded(y):
            return [image[y, x] for x in range(8)]

        def finish(upper, lower, p, totals):
            rows = mixed(upper, lower, p, ((0, 2), (1, 3)))
            for row, y in zip(rows, (2 * p, 2 * p + 1)):
                row = along_x(along_x_shifted(row, y), y)
                for x in range(8):
                    value = image[y, x] + pltpu.roll(row[x] * growth[y, x], 126, 1)
                    value = history[base, y, x] - size * value
                    gradient[y, x] = value
                    totals = add_squares(totals, x, value)
            return totals

        totals = [zero] * 4
        last, upper = across_halves(loaded(HALF_ROWS - 1), loaded(0))
        for x in range(8):
            edge[x] = last[x]
        for p in range(PAIRS - 1):
            lower, later = across(loaded(2 * p + 1), loaded(2 * p + 2), p)
            totals = finish(upper, lower, p, totals)
            upper = later
        return finish(upper, [edge[x] for x in range(8)], PAIRS - 1, totals)

    def whole(totals):
        return jnp.sum(sum(totals), keepdims=True)

    def turn(k, carry):
        gamma_before, totals = carry
        gamma = whole(totals)
        beta = jnp.where(k < 2, 0.0, gamma / gamma_before)
        beta = jnp.where(k == 0, -1.0, beta)
        squares = whole(forward_pass(k, beta))
        size = jnp.where(k == 0, 1.0, gamma / squares)
        betas[k] = jnp.broadcast_to(beta, (8, 128))
        steps[k] = jnp.broadcast_to(size, (8, 128))
        base = jnp.where(k == 0, ITERS + 1, k)
        return gamma, backward_pass(base, size)

    one = jnp.ones((8, 128), jnp.float32)
    lax.fori_loop(0, ITERS + 1, turn, (jnp.ones((1, 1), jnp.float32), [one] * 4))

    weights = [steps[ITERS]]
    for k in range(ITERS - 1, 0, -1):
        weights.insert(0, steps[k] + betas[k + 1] * weights[0])
    for q in range(8):
        mine = pl.ds(core * 16 + 2 * q, 2)
        total = history[0, mine]
        for k in range(1, ITERS + 1):
            total = total + weights[k - 1] * history[k, mine]
        out_ref[pl.ds(q, PANEL, stride=16), :] = total.reshape(128, 128).T
        block = gradient[mine].reshape(128, 128)
        out_ref[pl.ds(8 + q, PANEL, stride=16), :] = block.T


def unpack_kernel(arrived_ref, solution_ref, gradient_ref):
    for part, out_ref in enumerate((solution_ref, gradient_ref)):
        for q in range(8):
            block = arrived_ref[pl.ds(8 * part + q, PANEL, stride=16), :].T
            for y in range(2):
                for x in range(8):
                    i = y * 8 + x
                    out_ref[pl.ds((2 * q + y) * LX + x, 8, stride=8), :] = block[8 * i : 8 * i + 8]


def call(kernel, out_shape, scratch=(), smem_first=False, operands=1, cost=0):
    vmem = pl.BlockSpec(memory_space=pltpu.VMEM)
    in_specs = [vmem] * operands
    if smem_first:
        in_specs[0] = pl.BlockSpec(memory_space=pltpu.SMEM)
    return pl.pallas_call(
        kernel,
        out_shape=out_shape,
        in_specs=in_specs,
        out_specs=jax.tree.map(lambda _: vmem, out_shape),
        scratch_shapes=list(scratch),
        compiler_params=pltpu.CompilerParams(vmem_limit_bytes=VMEM_LIMIT),
        cost_estimate=pl.CostEstimate(flops=cost, bytes_accessed=1 << 20, transcendentals=0),
    )


def f32(*shape):
    return jax.ShapeDtypeStruct(shape, jnp.float32)


def exchange(values):
    parts = values.reshape(PANEL, 16, 128)
    moved = lax.all_to_all(parts, AXES, 0, 0, tiled=True, axis_index_groups=CORE_GROUPS)
    return moved.reshape(PANEL * 16, 128)


def local_solve(source_sites, own, other, bonds):
    tan, mix = call(
        tables_kernel,
        (f32(3, 128, 8, 128), f32(4, 128, 8, 128)),
        scratch=[
            pltpu.VMEM((4, 1024, 128), jnp.float32),
            pltpu.VMEM((2, 128, 8, 128), jnp.float32),
        ],
        cost=10_000_000,
    )(bonds)
    lattice = pltpu.VMEM((HALF_ROWS, 8, 8, 128), jnp.float32)
    return call(
        solve_kernel,
        f32(PANEL * 16, 128),
        scratch=[pltpu.VMEM((2048, 128), jnp.float32)]
        + [lattice] * 3
        + [pltpu.VMEM((ITERS + 2, HALF_ROWS, 8, 8, 128), jnp.float32)]
        + [lattice]
        + [pltpu.VMEM((8, 8, 128), jnp.float32)] * 3,
        smem_first=True,
        operands=5,
    )(source_sites, own, other, tan, mix)


def body(fields, bonds, source_sites, initial):
    packed = call(pack_kernel, f32(PANEL * 16, 128), operands=2)(
        initial.reshape(1024, PANEL), fields
    )
    own = exchange(packed)
    other = lax.ppermute(own, AXES, CORE_SWAP)
    solved = local_solve(source_sites, own, other, bonds)
    arrived = exchange(solved)
    solution, gradient = call(unpack_kernel, (f32(1024, PANEL), f32(1024, PANEL)))(arrived)
    return solution.reshape(1, 1024, PANEL), gradient.reshape(1, 1024, PANEL)


def solution(mesh):
    placed = (P("tm", "site"), P(), P(), P("tm", "site", None))
    return jax.shard_map(
        body,
        mesh=mesh,
        in_specs=placed,
        out_specs=(P("tm", "site", None), P("tm", "site", None)),
        check_vma=False,
    )
```

```python
import math

import jax
import jax.numpy as jnp
from jax import lax
from jax.experimental import pallas as pl
from jax.experimental.pallas import tpu as pltpu
from jax.sharding import PartitionSpec as P

LX = 64
LY = 64
PANEL = 128
SLICES = 64
ITERS = 6

coupling = 0.7368
hop_angle = 0.125

AXES = ("tm", "site")
TIMES = 64
STRIPS = 4
HALF_ROWS = LY // 2
PAIRS = HALF_ROWS // 2
CORE_GROUPS = [
    [t * STRIPS + 2 * half + core for t in range(TIMES) for half in range(2)] for core in range(2)
]
CORE_SWAP = [(i, i ^ 1) for i in range(TIMES * STRIPS)]
VMEM_LIMIT = 24 * 1024 * 1024


def pack_kernel(initial_ref, fields_ref, out_ref):
    sign = jnp.where(lax.axis_index("tm") == 0, 1.0, -1.0).astype(jnp.float32)
    for q in range(8):
        rows = [
            initial_ref[pl.ds((2 * q + y) * LX + x, 8, stride=8), :]
            for y in range(2)
            for x in range(8)
        ]
        out_ref[pl.ds(q, PANEL, stride=16), :] = jnp.concatenate(rows, axis=0).T
        spin = fields_ref[:, q * 128 : (q + 1) * 128].astype(jnp.float32)
        growth = sign * jnp.exp(coupling * (2.0 * spin - 1.0))
        out_ref[pl.ds(8 + q, PANEL, stride=16), :] = jnp.broadcast_to(growth, (PANEL, 128))


def tables_kernel(bonds_ref, tan_ref, mix_ref, flat_ref, cos_ref):
    cos_less = math.cosh(hop_angle) - 1.0
    tangent = math.tanh(hop_angle)
    odd = lax.broadcasted_iota(jnp.int32, (8, 128), 1) % 2 == 1
    upper = lax.broadcasted_iota(jnp.int32, (128, 128), 0) % 2 == 1
    for f in range(4):
        for q in range(8):
            low = bonds_ref[f : f + 1, q * 128 : (q + 1) * 128].astype(jnp.float32)
            high = bonds_ref[f : f + 1, 1024 + q * 128 : 1024 + (q + 1) * 128].astype(jnp.float32)
            both = jnp.where(
                upper, jnp.broadcast_to(high, (128, 128)), jnp.broadcast_to(low, (128, 128))
            )
            flat_ref[f, pl.ds(q * 128, 128), :] = both.T
        if f == 2:
            continue
        width = 4 if f < 2 else 8
        for i in range(128):
            start = (i // width) * width * 8 + i % width
            kept = flat_ref[f, pl.ds(start, 8, stride=width), :]
            tan_ref[f - f // 3, i] = kept * tangent
            if f > 0:
                cos_ref[f // 3, i] = 1.0 + kept * cos_less

    def cos_along(y, x):
        if x == 0:
            return pltpu.roll(cos_ref[0, y * 4 + 3], 1, 0)
        return cos_ref[0, y * 4 + (x - 1) // 2]

    for p in range(PAIRS):
        for x in range(8):
            kept = flat_ref[2, pl.ds(p * 64 + x, 8, stride=8), :]
            cos, sin = 1.0 + kept * cos_less, kept * math.sinh(hop_angle)
            if p == 0:
                before = swap_halves(cos_ref[1, (PAIRS - 1) * 8 + x], odd)
            else:
                before = cos_ref[1, (p - 1) * 8 + x]
            after = cos_ref[1, p * 8 + x]
            former, latter = cos_along(2 * p, x), cos_along(2 * p + 1, x)
            mix_ref[0, p * 8 + x] = before * cos * former
            mix_ref[1, p * 8 + x] = before * sin * latter
            mix_ref[2, p * 8 + x] = after * sin * former
            mix_ref[3, p * 8 + x] = after * cos * latter


def join(former, latter, tan):
    return former + tan * latter, latter + tan * former


def swap_halves(value, odd):
    return jnp.where(odd, pltpu.roll(value, 1, 1), pltpu.roll(value, 127, 1))


def arrange(core, source_ref, tan_ref, flat, start, growth, growth_before):
    for q in range(8):
        block = source_ref[pl.ds(q, PANEL, stride=16), :].T
        start[pl.ds(2 * q, 2)] = block.reshape(2, 8, 8, 128)
        block = source_ref[pl.ds(8 + q, PANEL, stride=16), :].T
        flat[pl.ds(q * 128, 128), :] = block
    for y in range(HALF_ROWS // 2):
        for x in range(8):
            bond = (core * 16 + y) * 4 + x // 2
            cos = jnp.where(tan_ref[0, bond] > 0.0, math.cosh(hop_angle), 1.0)
            value = flat[pl.ds(y * LX + x, 8, stride=8), :] * cos
            growth[y, x] = value
            growth_before[y, x] = pltpu.roll(value, 126, 1)


def arrange_kernel(own_ref, tan_ref, start, growth, growth_before, flat):
    core = lax.axis_index("site") % 2
    arrange(core, own_ref, tan_ref, flat, start, growth, growth_before)


def solve_kernel(
    sites_ref, own_start, own_growth, own_before, other_ref, tan_ref, mix_ref, out_ref,
    flat, growth, growth_before, gradient, history, image, edge, steps, betas,
):
    core = lax.axis_index("site") % 2
    column = 2 * lax.axis_index("tm") + lax.axis_index("site") // 2
    odd = lax.broadcasted_iota(jnp.int32, (8, 128), 1) % 2 == 1

    for y in range(HALF_ROWS // 2):
        own_y = core * 16 + y
        for x in range(8):
            gradient[own_y, x] = own_start[y, x]
            growth[own_y, x] = own_growth[y, x]
            growth_before[own_y, x] = own_before[y, x]
    other_rows = pl.ds((1 - core) * 16, 16)
    arrange(
        1 - core, other_ref, tan_ref, flat,
        gradient.at[other_rows], growth.at[other_rows], growth_before.at[other_rows],
    )
    zero = jnp.zeros((8, 128), jnp.float32)
    lane = lax.broadcasted_iota(jnp.int32, (8, 128), 1)
    chosen = jnp.where(lane[:1] == column, sites_ref[...].astype(jnp.float32), 0.0)
    site = jnp.sum(chosen, axis=1, keepdims=True).astype(jnp.int32)
    beside = lane % 2 * (HALF_ROWS * LX) + lax.broadcasted_iota(jnp.int32, (8, 128), 0) * 8
    wanted = jnp.where(lane // 2 == column * SLICES // PANEL, site - beside, -1)
    for y in range(HALF_ROWS):
        for x in range(8):
            image[y, x] = jnp.where(wanted == y * LX + x, 1.0, 0.0)
            history[ITERS + 1, y, x] = zero

    def along_x(row, y):
        row = list(row)
        for j in range(4):
            row[2 * j], row[2 * j + 1] = join(row[2 * j], row[2 * j + 1], tan_ref[0, y * 4 + j])
        return row

    def along_x_shifted(row, y):
        row = list(row)
        for j in range(3):
            row[2 * j + 1], row[2 * j + 2] = join(
                row[2 * j + 1], row[2 * j + 2], tan_ref[1, y * 4 + j]
            )
        row[7], wrapped = join(row[7], pltpu.roll(row[0], 7, 0), tan_ref[1, y * 4 + 3])
        row[0] = pltpu.roll(wrapped, 1, 0)
        return row

    def mixed(former, latter, pair, order):
        results = [[], []]
        for x in range(8):
            i = pair * 8 + x
            for side, (m, n) in enumerate(order):
                results[side].append(mix_ref[m, i] * former[x] + mix_ref[n, i] * latter[x])
        return results

    def across(former, latter, pair):
        results = [join(former[x], latter[x], tan_ref[2, pair * 8 + x]) for x in range(8)]
        return [r[0] for r in results], [r[1] for r in results]

    def across_halves(last, first):
        moved = [swap_halves(v, odd) for v in first]
        last, moved = across(last, moved, PAIRS - 1)
        return last, [swap_halves(v, odd) for v in moved]

    def add_squares(totals, x, value):
        totals = list(totals)
        totals[x % 4] = totals[x % 4] + value * value
        return totals

    def forward_pass(k, beta):
        def hopped(p):
            rows = []
            for y in (2 * p, 2 * p + 1):
                row = []
                for x in range(8):
                    value = gradient[y, x]
                    history[k, y, x] = value
                    row.append(value * growth_before[y, x])
                rows.append(along_x_shifted(along_x(row, y), y))
            return mixed(rows[0], rows[1], p, ((0, 1), (2, 3)))

        def put(row, y, totals):
            for x in range(8):
                value = (gradient[y, x] + pltpu.roll(row[x], 2, 1)) + beta * image[y, x]
                image[y, x] = value
                totals = add_squares(totals, x, value)
            return totals

        totals = [zero] * 4
        first, last = hopped(0)
        for x in range(8):
            edge[x] = first[x]
        for p in range(1, PAIRS):
            upper, lower = hopped(p)
            last, upper = across(last, upper, p - 1)
            totals = put(last, 2 * p - 1, totals)
            totals = put(upper, 2 * p, totals)
            last = lower
        last, first = across_halves(last, [edge[x] for x in range(8)])
        totals = put(last, HALF_ROWS - 1, totals)
        return put(first, 0, totals)

    def backward_pass(base, size):
        def loaded(y):
            return [image[y, x] for x in range(8)]

        def finish(upper, lower, p, totals):
            rows = mixed(upper, lower, p, ((0, 2), (1, 3)))
            for row, y in zip(rows, (2 * p, 2 * p + 1)):
                row = along_x(along_x_shifted(row, y), y)
                for x in range(8):
                    value = image[y, x] + pltpu.roll(row[x] * growth[y, x], 126, 1)
                    value = history[base, y, x] - size * value
                    gradient[y, x] = value
                    totals = add_squares(totals, x, value)
            return totals

        totals = [zero] * 4
        last, upper = across_halves(loaded(HALF_ROWS - 1), loaded(0))
        for x in range(8):
            edge[x] = last[x]
        for p in range(PAIRS - 1):
            lower, later = across(loaded(2 * p + 1), loaded(2 * p + 2), p)
            totals = finish(upper, lower, p, totals)
            upper = later
        return finish(upper, [edge[x] for x in range(8)], PAIRS - 1, totals)

    def whole(totals):
        return jnp.sum(sum(totals), keepdims=True)

    def turn(k, carry):
        gamma_before, totals = carry
        gamma = whole(totals)
        beta = jnp.where(k < 2, 0.0, gamma / gamma_before)
        beta = jnp.where(k == 0, -1.0, beta)
        squares = whole(forward_pass(k, beta))
        size = jnp.where(k == 0, 1.0, gamma / squares)
        betas[k] = jnp.broadcast_to(beta, (8, 128))
        steps[k] = jnp.broadcast_to(size, (8, 128))
        base = jnp.where(k == 0, ITERS + 1, k)
        return gamma, backward_pass(base, size)

    one = jnp.ones((8, 128), jnp.float32)
    lax.fori_loop(0, ITERS + 1, turn, (jnp.ones((1, 1), jnp.float32), [one] * 4))

    weights = [steps[ITERS]]
    for k in range(ITERS - 1, 0, -1):
        weights.insert(0, steps[k] + betas[k + 1] * weights[0])
    for q in range(8):
        mine = pl.ds(core * 16 + 2 * q, 2)
        total = history[0, mine]
        for k in range(1, ITERS + 1):
            total = total + weights[k - 1] * history[k, mine]
        out_ref[pl.ds(q, PANEL, stride=16), :] = total.reshape(128, 128).T
        block = gradient[mine].reshape(128, 128)
        out_ref[pl.ds(8 + q, PANEL, stride=16), :] = block.T


def unpack_kernel(arrived_ref, solution_ref, gradient_ref):
    for part, out_ref in enumerate((solution_ref, gradient_ref)):
        for q in range(8):
            block = arrived_ref[pl.ds(8 * part + q, PANEL, stride=16), :].T
            for y in range(2):
                for x in range(8):
                    i = y * 8 + x
                    out_ref[pl.ds((2 * q + y) * LX + x, 8, stride=8), :] = block[8 * i : 8 * i + 8]


def call(kernel, out_shape, scratch=(), operands=1, cost=0):
    vmem = pl.BlockSpec(memory_space=pltpu.VMEM)
    return pl.pallas_call(
        kernel,
        out_shape=out_shape,
        in_specs=[vmem] * operands,
        out_specs=jax.tree.map(lambda _: vmem, out_shape),
        scratch_shapes=list(scratch),
        compiler_params=pltpu.CompilerParams(vmem_limit_bytes=VMEM_LIMIT),
        cost_estimate=pl.CostEstimate(flops=cost, bytes_accessed=1 << 20, transcendentals=0),
    )


def f32(*shape):
    return jax.ShapeDtypeStruct(shape, jnp.float32)


def exchange(values):
    parts = values.reshape(PANEL, 16, 128)
    moved = lax.all_to_all(parts, AXES, 0, 0, tiled=True, axis_index_groups=CORE_GROUPS)
    return moved.reshape(PANEL * 16, 128)


def local_solve(source_sites, own, other, bonds):
    flat = pltpu.VMEM((1024, 128), jnp.float32)
    half = f32(HALF_ROWS // 2, 8, 8, 128)
    tan, mix = call(
        tables_kernel,
        (f32(3, 128, 8, 128), f32(4, 128, 8, 128)),
        scratch=[
            pltpu.VMEM((4, 1024, 128), jnp.float32),
            pltpu.VMEM((2, 128, 8, 128), jnp.float32),
        ],
        cost=10_000_000,
    )(bonds)
    arranged = call(arrange_kernel, (half, half, half), scratch=[flat], operands=2, cost=10_000_000)(
        own, tan
    )
    lattice = pltpu.VMEM((HALF_ROWS, 8, 8, 128), jnp.float32)
    return call(
        solve_kernel,
        f32(PANEL * 16, 128),
        scratch=[flat]
        + [lattice] * 3
        + [pltpu.VMEM((ITERS + 2, HALF_ROWS, 8, 8, 128), jnp.float32)]
        + [lattice]
        + [pltpu.VMEM((8, 8, 128), jnp.float32)] * 3,

        operands=7,
    )(source_sites.reshape(1, PANEL), *arranged, other, tan, mix)


def body(fields, bonds, source_sites, initial):
    packed = call(pack_kernel, f32(PANEL * 16, 128), operands=2)(
        initial.reshape(1024, PANEL), fields
    )
    own = exchange(packed)
    other = lax.ppermute(own, AXES, CORE_SWAP)
    solved = local_solve(source_sites, own, other, bonds)
    arrived = exchange(solved)
    solution, gradient = call(
        unpack_kernel,
        (f32(1024, PANEL), f32(1024, PANEL)),
    )(arrived)
    return solution.reshape(1, 1024, PANEL), gradient.reshape(1, 1024, PANEL)


def solution(mesh):
    placed = (P("tm", "site"), P(), P(), P("tm", "site", None))
    return jax.shard_map(
        body,
        mesh=mesh,
        in_specs=placed,
        out_specs=(P("tm", "site", None), P("tm", "site", None)),
        check_vma=False,
    )
```

```python
import math

import jax
import jax.numpy as jnp
from jax import lax
from jax.experimental import pallas as pl
from jax.experimental.pallas import tpu as pltpu
from jax.sharding import PartitionSpec as P

LX = 64
LY = 64
PANEL = 128
SLICES = 64
ITERS = 6

coupling = 0.7368
hop_angle = 0.125

AXES = ("tm", "site")
TIMES = 64
STRIPS = 4
HALF_ROWS = LY // 2
PAIRS = HALF_ROWS // 2
CORE_GROUPS = [
    [t * STRIPS + 2 * half + core for t in range(TIMES) for half in range(2)] for core in range(2)
]
CORE_SWAP = [(i, i ^ 1) for i in range(TIMES * STRIPS)]
VMEM_LIMIT = 24 * 1024 * 1024


def pack_kernel(initial_ref, growth_ref, out_ref):
    for q in range(8):
        rows = [
            initial_ref[pl.ds((2 * q + y) * LX + x, 8, stride=8), :]
            for y in range(2)
            for x in range(8)
        ]
        out_ref[pl.ds(q, PANEL, stride=16), :] = jnp.concatenate(rows, axis=0).T
        growth = growth_ref[:, q * 128 : (q + 1) * 128]
        out_ref[pl.ds(8 + q, PANEL, stride=16), :] = jnp.broadcast_to(growth, (PANEL, 128))


def tables_kernel(bonds_ref, tan_ref, mix_ref, flat_ref, cos_ref):
    cos_less = math.cosh(hop_angle) - 1.0
    tangent = math.tanh(hop_angle)
    odd = lax.broadcasted_iota(jnp.int32, (8, 128), 1) % 2 == 1
    upper = lax.broadcasted_iota(jnp.int32, (128, 128), 0) % 2 == 1
    for f in range(4):
        for q in range(8):
            low = bonds_ref[f : f + 1, q * 128 : (q + 1) * 128].astype(jnp.float32)
            high = bonds_ref[f : f + 1, 1024 + q * 128 : 1024 + (q + 1) * 128].astype(jnp.float32)
            both = jnp.where(
                upper, jnp.broadcast_to(high, (128, 128)), jnp.broadcast_to(low, (128, 128))
            )
            flat_ref[f, pl.ds(q * 128, 128), :] = both.T
        if f == 2:
            continue
        width = 4 if f < 2 else 8
        for i in range(128):
            start = (i // width) * width * 8 + i % width
            kept = flat_ref[f, pl.ds(start, 8, stride=width), :]
            tan_ref[f - f // 3, i] = kept * tangent
            if f > 0:
                cos_ref[f // 3, i] = 1.0 + kept * cos_less

    def cos_along(y, x):
        if x == 0:
            return pltpu.roll(cos_ref[0, y * 4 + 3], 1, 0)
        return cos_ref[0, y * 4 + (x - 1) // 2]

    for p in range(PAIRS):
        for x in range(8):
            kept = flat_ref[2, pl.ds(p * 64 + x, 8, stride=8), :]
            cos, sin = 1.0 + kept * cos_less, kept * math.sinh(hop_angle)
            if p == 0:
                before = swap_halves(cos_ref[1, (PAIRS - 1) * 8 + x], odd)
            else:
                before = cos_ref[1, (p - 1) * 8 + x]
            after = cos_ref[1, p * 8 + x]
            former, latter = cos_along(2 * p, x), cos_along(2 * p + 1, x)
            mix_ref[0, p * 8 + x] = before * cos * former
            mix_ref[1, p * 8 + x] = before * sin * latter
            mix_ref[2, p * 8 + x] = after * sin * former
            mix_ref[3, p * 8 + x] = after * cos * latter


def join(former, latter, tan):
    return former + tan * latter, latter + tan * former


def swap_halves(value, odd):
    return jnp.where(odd, pltpu.roll(value, 1, 1), pltpu.roll(value, 127, 1))


def arrange(core, source_ref, tan_ref, flat, start, growth, growth_before):
    for q in range(8):
        block = source_ref[pl.ds(q, PANEL, stride=16), :].T
        start[pl.ds(2 * q, 2)] = block.reshape(2, 8, 8, 128)
        block = source_ref[pl.ds(8 + q, PANEL, stride=16), :].T
        flat[pl.ds(q * 128, 128), :] = block
    for y in range(HALF_ROWS // 2):
        for x in range(8):
            bond = (core * 16 + y) * 4 + x // 2
            cos = jnp.where(tan_ref[0, bond] > 0.0, math.cosh(hop_angle), 1.0)
            value = flat[pl.ds(y * LX + x, 8, stride=8), :] * cos
            growth[y, x] = value
            growth_before[y, x] = pltpu.roll(value, 126, 1)


def arrange_kernel(own_ref, tan_ref, start, growth, growth_before, flat):
    core = lax.axis_index("site") % 2
    arrange(core, own_ref, tan_ref, flat, start, growth, growth_before)


def solve_kernel(
    sites_ref, own_start, own_growth, own_before, other_ref, tan_ref, mix_ref, out_ref,
    flat, growth, growth_before, gradient, history, image, edge, steps, betas,
):
    core = lax.axis_index("site") % 2
    column = 2 * lax.axis_index("tm") + lax.axis_index("site") // 2
    odd = lax.broadcasted_iota(jnp.int32, (8, 128), 1) % 2 == 1

    for y in range(HALF_ROWS // 2):
        own_y = core * 16 + y
        for x in range(8):
            gradient[own_y, x] = own_start[y, x]
            growth[own_y, x] = own_growth[y, x]
            growth_before[own_y, x] = own_before[y, x]
    other_rows = pl.ds((1 - core) * 16, 16)
    arrange(
        1 - core, other_ref, tan_ref, flat,
        gradient.at[other_rows], growth.at[other_rows], growth_before.at[other_rows],
    )
    zero = jnp.zeros((8, 128), jnp.float32)
    lane = lax.broadcasted_iota(jnp.int32, (8, 128), 1)
    chosen = jnp.where(lane[:1] == column, sites_ref[...].astype(jnp.float32), 0.0)
    site = jnp.sum(chosen, axis=1, keepdims=True).astype(jnp.int32)
    beside = lane % 2 * (HALF_ROWS * LX) + lax.broadcasted_iota(jnp.int32, (8, 128), 0) * 8
    wanted = jnp.where(lane // 2 == column * SLICES // PANEL, site - beside, -1)
    for y in range(HALF_ROWS):
        for x in range(8):
            image[y, x] = jnp.where(wanted == y * LX + x, 1.0, 0.0)
            history[ITERS + 1, y, x] = zero

    def along_x(row, y):
        row = list(row)
        for j in range(4):
            row[2 * j], row[2 * j + 1] = join(row[2 * j], row[2 * j + 1], tan_ref[0, y * 4 + j])
        return row

    def along_x_shifted(row, y):
        row = list(row)
        for j in range(3):
            row[2 * j + 1], row[2 * j + 2] = join(
                row[2 * j + 1], row[2 * j + 2], tan_ref[1, y * 4 + j]
            )
        row[7], wrapped = join(row[7], pltpu.roll(row[0], 7, 0), tan_ref[1, y * 4 + 3])
        row[0] = pltpu.roll(wrapped, 1, 0)
        return row

    def mixed(former, latter, pair, order):
        results = [[], []]
        for x in range(8):
            i = pair * 8 + x
            for side, (m, n) in enumerate(order):
                results[side].append(mix_ref[m, i] * former[x] + mix_ref[n, i] * latter[x])
        return results

    def across(former, latter, pair):
        results = [join(former[x], latter[x], tan_ref[2, pair * 8 + x]) for x in range(8)]
        return [r[0] for r in results], [r[1] for r in results]

    def across_halves(last, first):
        moved = [swap_halves(v, odd) for v in first]
        last, moved = across(last, moved, PAIRS - 1)
        return last, [swap_halves(v, odd) for v in moved]

    def add_squares(totals, x, value):
        totals = list(totals)
        totals[x] = totals[x] + value * value
        return totals

    def forward_pass(k, beta):
        def hopped(p):
            rows = []
            for y in (2 * p, 2 * p + 1):
                row = []
                for x in range(8):
                    value = gradient[y, x]
                    history[k, y, x] = value
                    row.append(value * growth_before[y, x])
                rows.append(along_x_shifted(along_x(row, y), y))
            return mixed(rows[0], rows[1], p, ((0, 1), (2, 3)))

        def put(row, y, totals):
            for x in range(8):
                value = (gradient[y, x] + beta * image[y, x]) + pltpu.roll(row[x], 2, 1)
                image[y, x] = value
                totals = add_squares(totals, x, value)
            return totals

        totals = [zero] * 8
        first, last = hopped(0)
        for x in range(8):
            edge[x] = first[x]
        for p in range(1, PAIRS):
            upper, lower = hopped(p)
            last, upper = across(last, upper, p - 1)
            totals = put(last, 2 * p - 1, totals)
            totals = put(upper, 2 * p, totals)
            last = lower
        last, first = across_halves(last, [edge[x] for x in range(8)])
        totals = put(last, HALF_ROWS - 1, totals)
        return put(first, 0, totals)

    def backward_pass(base, size):
        def loaded(y):
            return [image[y, x] for x in range(8)]

        def finish(upper, lower, p, totals):
            rows = mixed(upper, lower, p, ((0, 2), (1, 3)))
            for row, y in zip(rows, (2 * p, 2 * p + 1)):
                row = along_x(along_x_shifted(row, y), y)
                for x in range(8):
                    value = image[y, x] + pltpu.roll(row[x] * growth[y, x], 126, 1)
                    value = history[base, y, x] - size * value
                    gradient[y, x] = value
                    totals = add_squares(totals, x, value)
            return totals

        totals = [zero] * 8
        last, upper = across_halves(loaded(HALF_ROWS - 1), loaded(0))
        for x in range(8):
            edge[x] = last[x]
        for p in range(PAIRS - 1):
            lower, later = across(loaded(2 * p + 1), loaded(2 * p + 2), p)
            totals = finish(upper, lower, p, totals)
            upper = later
        return finish(upper, [edge[x] for x in range(8)], PAIRS - 1, totals)

    def whole(totals):
        return jnp.sum(sum(totals), keepdims=True)

    def turn(k, carry):
        gamma_before, totals = carry
        gamma = whole(totals)
        beta = jnp.where(k < 2, 0.0, gamma / gamma_before)
        beta = jnp.where(k == 0, -1.0, beta)
        squares = whole(forward_pass(k, beta))
        size = jnp.where(k == 0, 1.0, gamma / squares)
        betas[k] = jnp.broadcast_to(beta, (8, 128))
        steps[k] = jnp.broadcast_to(size, (8, 128))
        base = jnp.where(k == 0, ITERS + 1, k)
        return gamma, backward_pass(base, size)

    one = jnp.ones((8, 128), jnp.float32)
    lax.fori_loop(0, ITERS + 1, turn, (jnp.ones((1, 1), jnp.float32), [one] * 8))

    weights = [steps[ITERS]]
    for k in range(ITERS - 1, 0, -1):
        weights.insert(0, steps[k] + betas[k + 1] * weights[0])
    for q in range(8):
        mine = pl.ds(core * 16 + 2 * q, 2)
        total = history[0, mine]
        for k in range(1, ITERS + 1):
            total = total + weights[k - 1] * history[k, mine]
        out_ref[pl.ds(q, PANEL, stride=16), :] = total.reshape(128, 128).T
        block = gradient[mine].reshape(128, 128)
        out_ref[pl.ds(8 + q, PANEL, stride=16), :] = block.T


def unpack_kernel(arrived_ref, solution_ref, gradient_ref):
    for part, out_ref in enumerate((solution_ref, gradient_ref)):
        for q in range(8):
            block = arrived_ref[pl.ds(8 * part + q, PANEL, stride=16), :].T
            for y in range(2):
                for x in range(8):
                    i = y * 8 + x
                    out_ref[pl.ds((2 * q + y) * LX + x, 8, stride=8), :] = block[8 * i : 8 * i + 8]


def call(kernel, out_shape, scratch=(), operands=1, cost=0):
    vmem = pl.BlockSpec(memory_space=pltpu.VMEM)
    return pl.pallas_call(
        kernel,
        out_shape=out_shape,
        in_specs=[vmem] * operands,
        out_specs=jax.tree.map(lambda _: vmem, out_shape),
        scratch_shapes=list(scratch),
        compiler_params=pltpu.CompilerParams(vmem_limit_bytes=VMEM_LIMIT),
        cost_estimate=pl.CostEstimate(flops=cost, bytes_accessed=1 << 20, transcendentals=0),
    )


def f32(*shape):
    return jax.ShapeDtypeStruct(shape, jnp.float32)


def exchange(values):
    parts = values.reshape(PANEL, 16, 128)
    moved = lax.all_to_all(parts, AXES, 0, 0, tiled=True, axis_index_groups=CORE_GROUPS)
    return moved.reshape(PANEL * 16, 128)


def local_solve(source_sites, own, other, bonds):
    flat = pltpu.VMEM((1024, 128), jnp.float32)
    half = f32(HALF_ROWS // 2, 8, 8, 128)
    tan, mix = call(
        tables_kernel,
        (f32(3, 129, 8, 128), f32(4, 129, 8, 128)),
        scratch=[
            pltpu.VMEM((4, 1024, 128), jnp.float32),
            pltpu.VMEM((2, 128, 8, 128), jnp.float32),
        ],
        cost=10_000_000,
    )(bonds)
    arranged = call(arrange_kernel, (half, half, half), scratch=[flat], operands=2, cost=10_000_000)(
        own, tan
    )
    lattice = pltpu.VMEM((HALF_ROWS, 8, 8, 128), jnp.float32)
    return call(
        solve_kernel,
        f32(PANEL * 16, 128),
        scratch=[flat]
        + [lattice] * 3
        + [pltpu.VMEM((ITERS + 2, HALF_ROWS, 8, 8, 128), jnp.float32)]
        + [lattice]
        + [pltpu.VMEM((8, 8, 128), jnp.float32)] * 3,

        operands=7,
    )(source_sites.reshape(1, PANEL), *arranged, other, tan, mix)


def body(fields, bonds, source_sites, initial):
    sign = jnp.where(lax.axis_index("tm") == 0, 1.0, -1.0).astype(jnp.float32)
    growth = sign * jnp.exp(coupling * (2.0 * fields.astype(jnp.float32) - 1.0))
    packed = call(pack_kernel, f32(PANEL * 16, 128), operands=2)(
        initial.reshape(1024, PANEL), growth
    )
    own = exchange(packed)
    other = lax.ppermute(own, AXES, CORE_SWAP)
    solved = local_solve(source_sites, own, other, bonds)
    arrived = exchange(solved)
    solution, gradient = call(
        unpack_kernel,
        (f32(1024, PANEL), f32(1024, PANEL)),
    )(arrived)
    return solution.reshape(1, 1024, PANEL), gradient.reshape(1, 1024, PANEL)


def solution(mesh):
    placed = (P("tm", "site"), P(), P(), P("tm", "site", None))
    return jax.shard_map(
        body,
        mesh=mesh,
        in_specs=placed,
        out_specs=(P("tm", "site", None), P("tm", "site", None)),
        check_vma=False,
    )
```

```python
import math

import jax
import jax.numpy as jnp
from jax import lax
from jax.experimental import pallas as pl
from jax.experimental.pallas import tpu as pltpu
from jax.sharding import PartitionSpec as P

LX = 64
LY = 64
PANEL = 128
SLICES = 64
ITERS = 6

coupling = 0.7368
hop_angle = 0.125

AXES = ("tm", "site")
TIMES = 64
STRIPS = 4
HALF_ROWS = LY // 2
PAIRS = HALF_ROWS // 2
CORE_GROUPS = [
    [t * STRIPS + 2 * half + core for t in range(TIMES) for half in range(2)] for core in range(2)
]
CORE_SWAP = [(i, i ^ 1) for i in range(TIMES * STRIPS)]
VMEM_LIMIT = 24 * 1024 * 1024


def pack_kernel(initial_ref, growth_ref, out_ref):
    for q in range(8):
        rows = [
            initial_ref[pl.ds((2 * q + y) * LX + x, 8, stride=8), :]
            for y in range(2)
            for x in range(8)
        ]
        out_ref[pl.ds(q, PANEL, stride=16), :] = jnp.concatenate(rows, axis=0).T
        growth = growth_ref[:, q * 128 : (q + 1) * 128]
        out_ref[pl.ds(8 + q, PANEL, stride=16), :] = jnp.broadcast_to(growth, (PANEL, 128))


def tables_kernel(bonds_ref, tan_ref, mix_ref, flat_ref, cos_ref):
    cos_less = math.cosh(hop_angle) - 1.0
    tangent = math.tanh(hop_angle)
    odd = lax.broadcasted_iota(jnp.int32, (8, 128), 1) % 2 == 1
    upper = lax.broadcasted_iota(jnp.int32, (128, 128), 0) % 2 == 1
    for f in range(4):
        for q in range(8):
            low = bonds_ref[f : f + 1, q * 128 : (q + 1) * 128].astype(jnp.float32)
            high = bonds_ref[f : f + 1, 1024 + q * 128 : 1024 + (q + 1) * 128].astype(jnp.float32)
            both = jnp.where(
                upper, jnp.broadcast_to(high, (128, 128)), jnp.broadcast_to(low, (128, 128))
            )
            flat_ref[f, pl.ds(q * 128, 128), :] = both.T
        if f == 2:
            continue
        width = 4 if f < 2 else 8
        for i in range(128):
            start = (i // width) * width * 8 + i % width
            kept = flat_ref[f, pl.ds(start, 8, stride=width), :]
            tan_ref[f - f // 3, i] = kept * tangent
            if f > 0:
                cos_ref[f // 3, i] = 1.0 + kept * cos_less

    def cos_along(y, x):
        if x == 0:
            return pltpu.roll(cos_ref[0, y * 4 + 3], 1, 0)
        return cos_ref[0, y * 4 + (x - 1) // 2]

    for p in range(PAIRS):
        for x in range(8):
            kept = flat_ref[2, pl.ds(p * 64 + x, 8, stride=8), :]
            cos, sin = 1.0 + kept * cos_less, kept * math.sinh(hop_angle)
            if p == 0:
                before = swap_halves(cos_ref[1, (PAIRS - 1) * 8 + x], odd)
            else:
                before = cos_ref[1, (p - 1) * 8 + x]
            after = cos_ref[1, p * 8 + x]
            former, latter = cos_along(2 * p, x), cos_along(2 * p + 1, x)
            mix_ref[0, p * 8 + x] = before * cos * former
            mix_ref[1, p * 8 + x] = before * sin * latter
            mix_ref[2, p * 8 + x] = after * sin * former
            mix_ref[3, p * 8 + x] = after * cos * latter


def join(former, latter, tan):
    return former + tan * latter, latter + tan * former


def swap_halves(value, odd):
    return jnp.where(odd, pltpu.roll(value, 1, 1), pltpu.roll(value, 127, 1))


def arrange(core, source_ref, tan_ref, flat, start, growth, growth_before):
    for q in range(8):
        block = source_ref[pl.ds(q, PANEL, stride=16), :].T
        start[pl.ds(2 * q, 2)] = block.reshape(2, 8, 8, 128)
        block = source_ref[pl.ds(8 + q, PANEL, stride=16), :].T
        flat[pl.ds(q * 128, 128), :] = block
    for y in range(HALF_ROWS // 2):
        for x in range(8):
            bond = (core * 16 + y) * 4 + x // 2
            cos = jnp.where(tan_ref[0, bond] > 0.0, math.cosh(hop_angle), 1.0)
            value = flat[pl.ds(y * LX + x, 8, stride=8), :] * cos
            growth[y, x] = value
            growth_before[y, x] = pltpu.roll(value, 126, 1)


def arrange_kernel(own_ref, tan_ref, start, growth, growth_before, flat):
    core = lax.axis_index("site") % 2
    arrange(core, own_ref, tan_ref, flat, start, growth, growth_before)


def solve_kernel(
    sites_ref, own_start, own_growth, own_before, other_ref, tan_ref, mix_ref, out_ref,
    flat, growth, growth_before, start, odd_turns, even_turns, image, edge, steps, betas,
):
    core = lax.axis_index("site") % 2
    column = 2 * lax.axis_index("tm") + lax.axis_index("site") // 2
    odd = lax.broadcasted_iota(jnp.int32, (8, 128), 1) % 2 == 1

    for y in range(HALF_ROWS // 2):
        own_y = core * 16 + y
        for x in range(8):
            start[own_y, x] = own_start[y, x]
            growth[own_y, x] = own_growth[y, x]
            growth_before[own_y, x] = own_before[y, x]
    other_rows = pl.ds((1 - core) * 16, 16)
    arrange(
        1 - core, other_ref, tan_ref, flat,
        start.at[other_rows], growth.at[other_rows], growth_before.at[other_rows],
    )
    zero = jnp.zeros((8, 128), jnp.float32)
    lane = lax.broadcasted_iota(jnp.int32, (8, 128), 1)
    chosen = jnp.where(lane[:1] == column, sites_ref[...].astype(jnp.float32), 0.0)
    site = jnp.sum(chosen, axis=1, keepdims=True).astype(jnp.int32)
    beside = lane % 2 * (HALF_ROWS * LX) + lax.broadcasted_iota(jnp.int32, (8, 128), 0) * 8
    wanted = jnp.where(lane // 2 == column * SLICES // PANEL, site - beside, -1)
    for y in range(HALF_ROWS):
        for x in range(8):
            image[y, x] = jnp.where(wanted == y * LX + x, 1.0, 0.0)

    def along_x(row, y):
        row = list(row)
        for j in range(4):
            row[2 * j], row[2 * j + 1] = join(row[2 * j], row[2 * j + 1], tan_ref[0, y * 4 + j])
        return row

    def along_x_shifted(row, y):
        row = list(row)
        for j in range(3):
            row[2 * j + 1], row[2 * j + 2] = join(
                row[2 * j + 1], row[2 * j + 2], tan_ref[1, y * 4 + j]
            )
        row[7], wrapped = join(row[7], pltpu.roll(row[0], 7, 0), tan_ref[1, y * 4 + 3])
        row[0] = pltpu.roll(wrapped, 1, 0)
        return row

    def mixed(former, latter, pair, order):
        results = [[], []]
        for x in range(8):
            i = pair * 8 + x
            for side, (m, n) in enumerate(order):
                results[side].append(mix_ref[m, i] * former[x] + mix_ref[n, i] * latter[x])
        return results

    def across(former, latter, pair):
        results = [join(former[x], latter[x], tan_ref[2, pair * 8 + x]) for x in range(8)]
        return [r[0] for r in results], [r[1] for r in results]

    def across_halves(last, first):
        moved = [swap_halves(v, odd) for v in first]
        last, moved = across(last, moved, PAIRS - 1)
        return last, [swap_halves(v, odd) for v in moved]

    def add_squares(totals, x, value):
        totals = list(totals)
        totals[x] = totals[x] + value * value
        return totals

    def forward_pass(source, beta):
        def hopped(p):
            rows = []
            for y in (2 * p, 2 * p + 1):
                row = []
                for x in range(8):
                    row.append(source[y, x] * growth_before[y, x])
                rows.append(along_x_shifted(along_x(row, y), y))
            return mixed(rows[0], rows[1], p, ((0, 1), (2, 3)))

        def put(row, y, totals):
            for x in range(8):
                value = (source[y, x] + beta * image[y, x]) + pltpu.roll(row[x], 2, 1)
                image[y, x] = value
                totals = add_squares(totals, x, value)
            return totals

        totals = [zero] * 8
        first, last = hopped(0)
        for x in range(8):
            edge[x] = first[x]
        for p in range(1, PAIRS):
            upper, lower = hopped(p)
            last, upper = across(last, upper, p - 1)
            totals = put(last, 2 * p - 1, totals)
            totals = put(upper, 2 * p, totals)
            last = lower
        last, first = across_halves(last, [edge[x] for x in range(8)])
        totals = put(last, HALF_ROWS - 1, totals)
        return put(first, 0, totals)

    def backward_pass(source, target, size):
        def loaded(y):
            return [image[y, x] for x in range(8)]

        def finish(upper, lower, p, totals):
            rows = mixed(upper, lower, p, ((0, 2), (1, 3)))
            for row, y in zip(rows, (2 * p, 2 * p + 1)):
                row = along_x(along_x_shifted(row, y), y)
                for x in range(8):
                    value = image[y, x] + pltpu.roll(row[x] * growth[y, x], 126, 1)
                    value = -value if source is None else source[y, x] - size * value
                    target[y, x] = value
                    totals = add_squares(totals, x, value)
            return totals

        totals = [zero] * 8
        last, upper = across_halves(loaded(HALF_ROWS - 1), loaded(0))
        for x in range(8):
            edge[x] = last[x]
        for p in range(PAIRS - 1):
            lower, later = across(loaded(2 * p + 1), loaded(2 * p + 2), p)
            totals = finish(upper, lower, p, totals)
            upper = later
        return finish(upper, [edge[x] for x in range(8)], PAIRS - 1, totals)

    def whole(totals):
        return jnp.sum(sum(totals), keepdims=True)

    def turn(k, source, target, gamma, beta):
        size = gamma / whole(forward_pass(source, beta))
        betas[k] = jnp.broadcast_to(beta, (8, 128))
        steps[k] = jnp.broadcast_to(size, (8, 128))
        return backward_pass(source, target, size)

    def two_turns(j, carry):
        gamma_before, totals = carry
        gamma = whole(totals)
        beta = jnp.where(j == 0, 0.0, gamma / gamma_before)
        totals = turn(2 * j + 1, odd_turns.at[j], even_turns.at[j], gamma, beta)
        gamma_next = whole(totals)
        beta = gamma_next / gamma
        return gamma_next, turn(
            2 * j + 2, even_turns.at[j], odd_turns.at[j + 1], gamma_next, beta
        )

    forward_pass(start, -1.0)
    totals = backward_pass(None, odd_turns.at[0], None)
    lax.fori_loop(0, ITERS // 2, two_turns, (jnp.ones((1, 1), jnp.float32), totals))

    weights = [steps[ITERS]]
    for k in range(ITERS - 1, 0, -1):
        weights.insert(0, steps[k] + betas[k + 1] * weights[0])
    for q in range(8):
        mine = pl.ds(core * 16 + 2 * q, 2)
        total = start[mine]
        for k in range(1, ITERS + 1):
            turns = odd_turns if k % 2 else even_turns
            total = total + weights[k - 1] * turns[(k - 1) // 2, mine]
        out_ref[pl.ds(q, PANEL, stride=16), :] = total.reshape(128, 128).T
        block = odd_turns[ITERS // 2, mine].reshape(128, 128)
        out_ref[pl.ds(8 + q, PANEL, stride=16), :] = block.T


def unpack_kernel(arrived_ref, solution_ref, gradient_ref):
    for part, out_ref in enumerate((solution_ref, gradient_ref)):
        for q in range(8):
            block = arrived_ref[pl.ds(8 * part + q, PANEL, stride=16), :].T
            for y in range(2):
                for x in range(8):
                    i = y * 8 + x
                    out_ref[pl.ds((2 * q + y) * LX + x, 8, stride=8), :] = block[8 * i : 8 * i + 8]


def call(kernel, out_shape, scratch=(), operands=1, cost=0):
    vmem = pl.BlockSpec(memory_space=pltpu.VMEM)
    return pl.pallas_call(
        kernel,
        out_shape=out_shape,
        in_specs=[vmem] * operands,
        out_specs=jax.tree.map(lambda _: vmem, out_shape),
        scratch_shapes=list(scratch),
        compiler_params=pltpu.CompilerParams(vmem_limit_bytes=VMEM_LIMIT),
        cost_estimate=pl.CostEstimate(flops=cost, bytes_accessed=1 << 20, transcendentals=0),
    )


def f32(*shape):
    return jax.ShapeDtypeStruct(shape, jnp.float32)


def exchange(values):
    parts = values.reshape(PANEL, 16, 128)
    moved = lax.all_to_all(parts, AXES, 0, 0, tiled=True, axis_index_groups=CORE_GROUPS)
    return moved.reshape(PANEL * 16, 128)


def local_solve(source_sites, own, other, bonds):
    flat = pltpu.VMEM((1024, 128), jnp.float32)
    half = f32(HALF_ROWS // 2, 8, 8, 128)
    tan, mix = call(
        tables_kernel,
        (f32(3, 129, 8, 128), f32(4, 129, 8, 128)),
        scratch=[
            pltpu.VMEM((4, 1024, 128), jnp.float32),
            pltpu.VMEM((2, 128, 8, 128), jnp.float32),
        ],
        cost=10_000_000,
    )(bonds)
    arranged = call(arrange_kernel, (half, half, half), scratch=[flat], operands=2, cost=10_000_000)(
        own, tan
    )
    lattice = pltpu.VMEM((HALF_ROWS, 8, 8, 128), jnp.float32)
    return call(
        solve_kernel,
        f32(PANEL * 16, 128),
        scratch=[flat]
        + [lattice] * 3
        + [pltpu.VMEM((n, HALF_ROWS, 8, 8, 128), jnp.float32) for n in (ITERS // 2 + 1, ITERS // 2)]
        + [lattice]
        + [pltpu.VMEM((8, 8, 128), jnp.float32)] * 3,
        operands=7,
    )(source_sites.reshape(1, PANEL), *arranged, other, tan, mix)


def body(fields, bonds, source_sites, initial):
    sign = jnp.where(lax.axis_index("tm") == 0, 1.0, -1.0).astype(jnp.float32)
    growth = sign * jnp.exp(coupling * (2.0 * fields.astype(jnp.float32) - 1.0))
    packed = call(pack_kernel, f32(PANEL * 16, 128), operands=2)(
        initial.reshape(1024, PANEL), growth
    )
    own = exchange(packed)
    other = lax.ppermute(own, AXES, CORE_SWAP)
    solved = local_solve(source_sites, own, other, bonds)
    arrived = exchange(solved)
    solution, gradient = call(
        unpack_kernel,
        (f32(1024, PANEL), f32(1024, PANEL)),
    )(arrived)
    return solution.reshape(1, 1024, PANEL), gradient.reshape(1, 1024, PANEL)


def solution(mesh):
    placed = (P("tm", "site"), P(), P(), P("tm", "site", None))
    return jax.shard_map(
        body,
        mesh=mesh,
        in_specs=placed,
        out_specs=(P("tm", "site", None), P("tm", "site", None)),
        check_vma=False,
    )
```

```python
import math

import jax
import jax.numpy as jnp
from jax import lax
from jax.experimental import pallas as pl
from jax.experimental.pallas import tpu as pltpu
from jax.sharding import PartitionSpec as P

LX = 64
LY = 64
PANEL = 128
SLICES = 64
ITERS = 6

coupling = 0.7368
hop_angle = 0.125

AXES = ("tm", "site")
TIMES = 64
STRIPS = 4
HALF_ROWS = LY // 2
PAIRS = HALF_ROWS // 2
CORE_GROUPS = [
    [t * STRIPS + 2 * half + core for t in range(TIMES) for half in range(2)] for core in range(2)
]
CORE_SWAP = [(i, i ^ 1) for i in range(TIMES * STRIPS)]
VMEM_LIMIT = 24 * 1024 * 1024


def pack_kernel(initial_ref, growth_ref, out_ref):
    for q in range(8):
        rows = [
            initial_ref[pl.ds((2 * q + y) * LX + x, 8, stride=8), :]
            for y in range(2)
            for x in range(8)
        ]
        out_ref[pl.ds(q, PANEL, stride=16), :] = jnp.concatenate(rows, axis=0).T
        growth = growth_ref[:, q * 128 : (q + 1) * 128]
        out_ref[pl.ds(8 + q, PANEL, stride=16), :] = jnp.broadcast_to(growth, (PANEL, 128))


def tables_kernel(bonds_ref, tan_ref, mix_ref, flat_ref, cos_ref):
    cos_less = math.cosh(hop_angle) - 1.0
    tangent = math.tanh(hop_angle)
    odd = lax.broadcasted_iota(jnp.int32, (8, 128), 1) % 2 == 1
    upper = lax.broadcasted_iota(jnp.int32, (128, 128), 0) % 2 == 1
    for f in range(4):
        for q in range(8):
            low = bonds_ref[f : f + 1, q * 128 : (q + 1) * 128].astype(jnp.float32)
            high = bonds_ref[f : f + 1, 1024 + q * 128 : 1024 + (q + 1) * 128].astype(jnp.float32)
            both = jnp.where(
                upper, jnp.broadcast_to(high, (128, 128)), jnp.broadcast_to(low, (128, 128))
            )
            flat_ref[f, pl.ds(q * 128, 128), :] = both.T
        if f == 2:
            continue
        width = 4 if f < 2 else 8
        for i in range(128):
            start = (i // width) * width * 8 + i % width
            kept = flat_ref[f, pl.ds(start, 8, stride=width), :]
            tan_ref[f - f // 3, i] = kept * tangent
            if f > 0:
                cos_ref[f // 3, i] = 1.0 + kept * cos_less

    def cos_along(y, x):
        if x == 0:
            return pltpu.roll(cos_ref[0, y * 4 + 3], 1, 0)
        return cos_ref[0, y * 4 + (x - 1) // 2]

    for p in range(PAIRS):
        for x in range(8):
            kept = flat_ref[2, pl.ds(p * 64 + x, 8, stride=8), :]
            cos, sin = 1.0 + kept * cos_less, kept * math.sinh(hop_angle)
            if p == 0:
                before = swap_halves(cos_ref[1, (PAIRS - 1) * 8 + x], odd)
            else:
                before = cos_ref[1, (p - 1) * 8 + x]
            after = cos_ref[1, p * 8 + x]
            former, latter = cos_along(2 * p, x), cos_along(2 * p + 1, x)
            mix_ref[0, p * 8 + x] = before * cos * former
            mix_ref[1, p * 8 + x] = before * sin * latter
            mix_ref[2, p * 8 + x] = after * sin * former
            mix_ref[3, p * 8 + x] = after * cos * latter


def join(former, latter, tan):
    return former + tan * latter, latter + tan * former


def swap_halves(value, odd):
    return jnp.where(odd, pltpu.roll(value, 1, 1), pltpu.roll(value, 127, 1))


def arrange(core, source_ref, tan_ref, flat, start, growth, growth_before):
    for q in range(8):
        block = source_ref[pl.ds(q, PANEL, stride=16), :].T
        start[pl.ds(2 * q, 2)] = block.reshape(2, 8, 8, 128)
        block = source_ref[pl.ds(8 + q, PANEL, stride=16), :].T
        flat[pl.ds(q * 128, 128), :] = block
    for y in range(HALF_ROWS // 2):
        for x in range(8):
            bond = (core * 16 + y) * 4 + x // 2
            cos = jnp.where(tan_ref[0, bond] > 0.0, math.cosh(hop_angle), 1.0)
            value = flat[pl.ds(y * LX + x, 8, stride=8), :] * cos
            growth[y, x] = value
            growth_before[y, x] = pltpu.roll(value, 126, 1)


def arrange_kernel(own_ref, tan_ref, start, growth, growth_before, flat):
    core = lax.axis_index("site") % 2
    arrange(core, own_ref, tan_ref, flat, start, growth, growth_before)


def solve_kernel(
    sites_ref, own_start, own_growth, own_before, other_ref, tan_ref, mix_ref, out_ref,
    flat, growth, growth_before, start, odd_turns, even_turns, image, edge, steps, betas,
):
    core = lax.axis_index("site") % 2
    column = 2 * lax.axis_index("tm") + lax.axis_index("site") // 2
    odd = lax.broadcasted_iota(jnp.int32, (8, 128), 1) % 2 == 1

    for y in range(HALF_ROWS // 2):
        own_y = core * 16 + y
        for x in range(8):
            start[own_y, x] = own_start[y, x]
            growth[own_y, x] = own_growth[y, x]
            growth_before[own_y, x] = own_before[y, x]
    other_rows = pl.ds((1 - core) * 16, 16)
    arrange(
        1 - core, other_ref, tan_ref, flat,
        start.at[other_rows], growth.at[other_rows], growth_before.at[other_rows],
    )
    zero = jnp.zeros((8, 128), jnp.float32)
    lane = lax.broadcasted_iota(jnp.int32, (8, 128), 1)
    chosen = jnp.where(lane[:1] == column, sites_ref[...].astype(jnp.float32), 0.0)
    site = jnp.sum(chosen, axis=1, keepdims=True).astype(jnp.int32)
    beside = lane % 2 * (HALF_ROWS * LX) + lax.broadcasted_iota(jnp.int32, (8, 128), 0) * 8
    wanted = jnp.where(lane // 2 == column * SLICES // PANEL, site - beside, -1)
    for y in range(HALF_ROWS):
        for x in range(8):
            image[y, x] = jnp.where(wanted == y * LX + x, 1.0, 0.0)

    def along_x(row, y):
        row = list(row)
        for j in range(4):
            row[2 * j], row[2 * j + 1] = join(row[2 * j], row[2 * j + 1], tan_ref[0, y * 4 + j])
        return row

    def along_x_shifted(row, y):
        row = list(row)
        for j in range(3):
            row[2 * j + 1], row[2 * j + 2] = join(
                row[2 * j + 1], row[2 * j + 2], tan_ref[1, y * 4 + j]
            )
        row[7], wrapped = join(row[7], pltpu.roll(row[0], 7, 0), tan_ref[1, y * 4 + 3])
        row[0] = pltpu.roll(wrapped, 1, 0)
        return row

    def mixed(former, latter, pair, order):
        results = [[], []]
        for x in range(8):
            i = pair * 8 + x
            for side, (m, n) in enumerate(order):
                results[side].append(mix_ref[m, i] * former[x] + mix_ref[n, i] * latter[x])
        return results

    def across(former, latter, pair):
        results = [join(former[x], latter[x], tan_ref[2, pair * 8 + x]) for x in range(8)]
        return [r[0] for r in results], [r[1] for r in results]

    def across_halves(last, first):
        moved = [swap_halves(v, odd) for v in first]
        last, moved = across(last, moved, PAIRS - 1)
        return last, [swap_halves(v, odd) for v in moved]

    def add_squares(totals, x, value):
        totals = list(totals)
        totals[x] = totals[x] + value * value
        return totals

    def forward_pass(source, beta):
        def hopped(p):
            rows = []
            for y in (2 * p, 2 * p + 1):
                row = []
                for x in range(8):
                    row.append(source[y, x] * growth_before[y, x])
                rows.append(along_x_shifted(along_x(row, y), y))
            return mixed(rows[0], rows[1], p, ((0, 1), (2, 3)))

        def put(row, y, totals):
            for x in range(8):
                value = (source[y, x] + beta * image[y, x]) + pltpu.roll(row[x], 2, 1)
                image[y, x] = value
                totals = add_squares(totals, x, value)
            return totals

        totals = [zero] * 8
        first, last = hopped(0)
        for x in range(8):
            edge[x] = first[x]
        for p in range(1, PAIRS):
            upper, lower = hopped(p)
            last, upper = across(last, upper, p - 1)
            totals = put(last, 2 * p - 1, totals)
            totals = put(upper, 2 * p, totals)
            last = lower
        last, first = across_halves(last, [edge[x] for x in range(8)])
        totals = put(last, HALF_ROWS - 1, totals)
        return put(first, 0, totals)

    def backward_pass(source, target, size):
        def loaded(y):
            return [image[y, x] for x in range(8)]

        def finish(upper, lower, p, totals):
            rows = mixed(upper, lower, p, ((0, 2), (1, 3)))
            for row, y in zip(rows, (2 * p, 2 * p + 1)):
                row = along_x(along_x_shifted(row, y), y)
                for x in range(8):
                    value = image[y, x] + pltpu.roll(row[x] * growth[y, x], 126, 1)
                    value = -value if source is None else source[y, x] - size * value
                    target[y, x] = value
                    totals = add_squares(totals, x, value)
            return totals

        totals = [zero] * 8
        last, upper = across_halves(loaded(HALF_ROWS - 1), loaded(0))
        for x in range(8):
            edge[x] = last[x]
        for p in range(PAIRS - 1):
            lower, later = across(loaded(2 * p + 1), loaded(2 * p + 2), p)
            totals = finish(upper, lower, p, totals)
            upper = later
        return finish(upper, [edge[x] for x in range(8)], PAIRS - 1, totals)

    def whole(totals):
        return jnp.sum(sum(totals), keepdims=True)

    def turn(k, source, target, gamma, beta):
        size = gamma / whole(forward_pass(source, beta))
        betas[k] = jnp.broadcast_to(beta, (8, 128))
        steps[k] = jnp.broadcast_to(size, (8, 128))
        return backward_pass(source, target, size)

    def two_turns(j, carry):
        gamma_before, totals = carry
        gamma = whole(totals)
        beta = jnp.where(j == 0, 0.0, gamma / gamma_before)
        totals = turn(2 * j + 1, odd_turns.at[j], even_turns.at[j], gamma, beta)
        gamma_next = whole(totals)
        beta = gamma_next / gamma
        return gamma_next, turn(
            2 * j + 2, even_turns.at[j], odd_turns.at[j + 1], gamma_next, beta
        )

    forward_pass(start, -1.0)
    totals = backward_pass(None, odd_turns.at[0], None)
    lax.fori_loop(0, ITERS // 2, two_turns, (jnp.ones((1, 1), jnp.float32), totals))

    weights = [steps[ITERS]]
    for k in range(ITERS - 1, 0, -1):
        weights.insert(0, steps[k] + betas[k + 1] * weights[0])
    for q in range(8):
        mine = pl.ds(core * 16 + 2 * q, 2)
        total = start[mine]
        for k in range(1, ITERS + 1):
            turns = odd_turns if k % 2 else even_turns
            total = total + weights[k - 1] * turns[(k - 1) // 2, mine]
        out_ref[pl.ds(q, PANEL, stride=16), :] = total.reshape(128, 128).T
        block = odd_turns[ITERS // 2, mine].reshape(128, 128)
        out_ref[pl.ds(8 + q, PANEL, stride=16), :] = block.T


def unpack_kernel(arrived_ref, solution_hbm, gradient_hbm, solution_ref, gradient_ref, sent):
    copies = []
    for q in range(8):
        for part, (ref, hbm) in enumerate(
            ((solution_ref, solution_hbm), (gradient_ref, gradient_hbm))
        ):
            block = arrived_ref[pl.ds(8 * part + q, PANEL, stride=16), :].T
            for y in range(2):
                for x in range(8):
                    i = y * 8 + x
                    ref[pl.ds((2 * q + y) * LX + x, 8, stride=8), :] = block[8 * i : 8 * i + 8]
            rows = pl.ds(q * 128, 128)
            copies.append(pltpu.make_async_copy(ref.at[rows], hbm.at[rows], sent.at[part, q]))
            copies[-1].start()
    for copy in copies:
        copy.wait()


def call(kernel, out_shape, scratch=(), operands=1, cost=0, out_space=pltpu.VMEM):
    vmem = pl.BlockSpec(memory_space=pltpu.VMEM)
    return pl.pallas_call(
        kernel,
        out_shape=out_shape,
        in_specs=[vmem] * operands,
        out_specs=jax.tree.map(lambda _: pl.BlockSpec(memory_space=out_space), out_shape),
        scratch_shapes=list(scratch),
        compiler_params=pltpu.CompilerParams(vmem_limit_bytes=VMEM_LIMIT),
        cost_estimate=pl.CostEstimate(flops=cost, bytes_accessed=1 << 20, transcendentals=0),
    )


def f32(*shape):
    return jax.ShapeDtypeStruct(shape, jnp.float32)


def exchange(values):
    parts = values.reshape(PANEL, 16, 128)
    moved = lax.all_to_all(parts, AXES, 0, 0, tiled=True, axis_index_groups=CORE_GROUPS)
    return moved.reshape(PANEL * 16, 128)


def local_solve(source_sites, own, other, bonds):
    flat = pltpu.VMEM((1024, 128), jnp.float32)
    half = f32(HALF_ROWS // 2, 8, 8, 128)
    tan, mix = call(
        tables_kernel,
        (f32(3, 129, 8, 128), f32(4, 129, 8, 128)),
        scratch=[
            pltpu.VMEM((4, 1024, 128), jnp.float32),
            pltpu.VMEM((2, 128, 8, 128), jnp.float32),
        ],
        cost=10_000_000,
    )(bonds)
    arranged = call(arrange_kernel, (half, half, half), scratch=[flat], operands=2, cost=10_000_000)(
        own, tan
    )
    lattice = pltpu.VMEM((HALF_ROWS, 8, 8, 128), jnp.float32)
    return call(
        solve_kernel,
        f32(PANEL * 16, 128),
        scratch=[flat]
        + [lattice] * 3
        + [pltpu.VMEM((n, HALF_ROWS, 8, 8, 128), jnp.float32) for n in (ITERS // 2 + 1, ITERS // 2)]
        + [lattice]
        + [pltpu.VMEM((8, 8, 128), jnp.float32)] * 3,
        operands=7,
    )(source_sites.reshape(1, PANEL), *arranged, other, tan, mix)


def body(fields, bonds, source_sites, initial):
    sign = jnp.where(lax.axis_index("tm") == 0, 1.0, -1.0).astype(jnp.float32)
    growth = sign * jnp.exp(coupling * (2.0 * fields.astype(jnp.float32) - 1.0))
    packed = call(pack_kernel, f32(PANEL * 16, 128), operands=2)(
        initial.reshape(1024, PANEL), growth
    )
    own = exchange(packed)
    other = lax.ppermute(own, AXES, CORE_SWAP)
    solved = local_solve(source_sites, own, other, bonds)
    arrived = exchange(solved)
    block = pltpu.VMEM((1024, PANEL), jnp.float32)
    solution, gradient = call(
        unpack_kernel,
        (f32(1024, PANEL), f32(1024, PANEL)),
        scratch=[block, block, pltpu.SemaphoreType.DMA((2, 8))],
        out_space=pl.ANY,
    )(arrived)
    return solution.reshape(1, 1024, PANEL), gradient.reshape(1, 1024, PANEL)


def solution(mesh):
    placed = (P("tm", "site"), P(), P(), P("tm", "site", None))
    return jax.shard_map(
        body,
        mesh=mesh,
        in_specs=placed,
        out_specs=(P("tm", "site", None), P("tm", "site", None)),
        check_vma=False,
    )
```
